32 devices in a mesh: lat: 8 (over y, x, core), lev: 4 (over z).
Axes of the slice: x: 2, y: 2, z: 4, core: 2. Of those that a mesh axis runs over, the one named last changes fastest.
Arguments:
- fourier: bfloat16 [2560, 48, 256], P('lat', 'lev'), may hold values from -6 to 6
- table: int32 [128], replicated, may hold values from 0 to 127, each once
- legendre: bfloat16 [128, 2, 129, 1280], P(('lat', 'lev')), may hold values from -0.15625 to 0.15625
Outputs:
- spectral: bfloat16 [128, 2, 48, 129], P(('lat', 'lev'))
The draws below stay inside these ranges and needn't reach their ends.
Inputs may be any that keep to these rules, and one draw needn't show every extreme that they name: `table`: every pair index appears exactly once.
All inputs are finite; a program needn't handle non-finite values.
Results may differ from the reference program's by a relative error of at most 0.0051.
Values may be sent and summed in bfloat16 or wider, within the bound.
No kernel may reach another device: no remote copies, remote signals or barrier semaphores. Data moves between devices by JAX's collectives and lax.ppermute only.
A program may use at most 128 MiB of HBM per device.

```python
import jax
import jax.numpy as jnp
from jax import lax

NLAT = 2560
JH = 1280
PAIRS = 128
M = 256
R = 129
C = 48


def level_of(rng, extent, pieces, least, top_value):
    def one(dim, blocks):
        draws = jax.random.uniform(jax.random.fold_in(jax.random.fold_in(rng, 6), dim), (blocks,), jnp.float32, least / len(pieces), top_value / len(pieces))
        return jnp.repeat(jnp.exp(draws), extent[dim] // blocks).reshape((-1,) + (1,) * (len(extent) - dim - 1))

    factor_of = one(*pieces[0])
    for cut in pieces[1:]:
        factor_of = factor_of * one(*cut)
    return factor_of


def normal_values(own_key, dims, deviation, limit, shards=(), held_as=jnp.bfloat16):
    drawn = jax.random.normal(own_key, dims, jnp.float32) * deviation
    if len(shards) > 0:
        drawn = level_of(own_key, dims, shards, -0.22, 0.18) * drawn
    return jnp.clip(drawn, min=-limit, max=limit).astype(held_as)


def setup_inputs(seed: int = 0) -> dict:
    key_list = jax.random.split(jax.random.key(seed), 4)
    return {
        "fourier": normal_values(key_list[0], (NLAT, C, M), 1.0, 6.0, ((0, 8), (1, 4))),
        "table": jax.random.permutation(key_list[1], PAIRS).astype(jnp.int32),
        "legendre": normal_values(key_list[2], (PAIRS, 2, R, JH), JH ** -0.5, 0.15625, ((0, 32),)),
    }


def transform_pair(combined, pair_index, tables):
    columns = jnp.stack([pair_index, M - 1 - pair_index]).astype(jnp.int32)
    selected = jnp.take(combined, columns, axis=3).astype(jnp.float32)
    products = jnp.einsum("erj,ejcw->ewcr", tables.astype(jnp.float32), selected)
    parity = jnp.arange(2).astype(jnp.int32)
    row_counts = (M - pair_index - parity + 1) // 2
    first_member = jnp.arange(R).astype(jnp.int32)[None, :] < row_counts[:, None]
    return jnp.where(first_member[:, None, :], products[:, 0], products[:, 1]).astype(jnp.bfloat16)


def reference(fourier, table, legendre):
    northern = fourier[:JH].astype(jnp.float32)
    southern = fourier[JH:].astype(jnp.float32)
    combined = jnp.stack([(northern + southern).astype(jnp.bfloat16), (northern - southern).astype(jnp.bfloat16)])

    def per_slot(pair_entry):
        return transform_pair(combined, pair_entry[0], pair_entry[1])

    return lax.map(per_slot, (table, legendre))
```

```python
import functools

import jax
import jax.numpy as jnp
from jax import lax
from jax.experimental import pallas as pl
from jax.experimental.pallas import tpu as pltpu
from jax.sharding import PartitionSpec as P

NT = (((1,), (1,)), ((), ()))


def pick_kernel(table_ref, x_ref, out_ref, onehot):
    rows, width = onehot.shape

    @pl.when(pl.program_id(0) == 0)
    def _():
        pairs = table_ref.shape[1]
        row = lax.broadcasted_iota(jnp.int32, (rows, pairs), 0)
        lane = lax.broadcasted_iota(jnp.int32, (rows, pairs), 1)
        mine = jnp.where(lane == row // 2, table_ref[...], 0)
        pair = jnp.sum(mine, axis=1, keepdims=True)
        second = lax.broadcasted_iota(jnp.int32, (rows, 1), 0) % 2 == 1
        column = jnp.where(second, width - 1 - pair, pair)
        at = lax.broadcasted_iota(jnp.int32, (rows, width), 1)
        onehot[...] = jnp.where(at == column, 1.0, 0.0).astype(jnp.bfloat16)

    picked = lax.dot_general(onehot[...], x_ref[...], NT, preferred_element_type=jnp.float32)
    out_ref[...] = picked.astype(jnp.bfloat16).reshape(out_ref.shape)


def pick(table, x, devices, steps):
    length, width = x.shape
    block = length // steps
    per = width // devices
    return pl.pallas_call(
        pick_kernel,
        grid=(steps,),
        in_specs=[
            pl.BlockSpec((1, table.shape[0]), lambda i: (0, 0)),
            pl.BlockSpec((block, width), lambda i: (i, 0)),
        ],
        out_specs=pl.BlockSpec((devices, per, block), lambda i: (0, 0, i)),
        out_shape=jax.ShapeDtypeStruct((devices, per, length), jnp.bfloat16),
        scratch_shapes=[pltpu.VMEM((width, width), jnp.bfloat16)],
        compiler_params=pltpu.CompilerParams(vmem_limit_bytes=40 * 2**20),
    )(table.reshape(1, -1), x)


def transform_kernel(first_ref, arrived_ref, tables_ref, out_ref, held, total, *, lat_rows):
    channels = arrived_ref.shape[3] // lat_rows
    both = 2 * lat_rows
    for x in range(2):
        for lev in range(4):
            for c in range(0, channels, 2):
                at = (lev * channels + c) * 8
                for core in range(2):
                    sym, anti = [], []
                    for k in (c, c + 1):
                        lanes = pl.ds(k * lat_rows, lat_rows)
                        north = arrived_ref[2 * x + core, lev, :, lanes].astype(jnp.float32)
                        south = arrived_ref[4 + 2 * x + core, lev, :, lanes].astype(jnp.float32)
                        sym.append(north + south)
                        anti.append(north - south)
                    lanes = pl.ds(x * both + core * lat_rows, lat_rows)
                    held[0, at : at + 16, lanes] = jnp.concatenate(sym, 0).astype(jnp.bfloat16)
                    held[1, at : at + 16, lanes] = jnp.concatenate(anti, 0).astype(jnp.bfloat16)
    for s in range(4):
        for e in range(2):
            products = lax.dot_general(
                held[e], tables_ref[s, e], NT, preferred_element_type=jnp.float32
            )
            for at in range(0, products.shape[1], 128):
                width = min(128, products.shape[1] - at)
                total[at // 128, :, :width] = products[:, at : at + width]
                one = total[at // 128, pl.ds(2 * s, 4 * channels, stride=8), :]
                two = total[at // 128, pl.ds(2 * s + 1, 4 * channels, stride=8), :]
                degree = lax.broadcasted_iota(jnp.int32, one.shape, 1) + at
                chosen = jnp.where(degree < first_ref[s, e], one, two).astype(jnp.bfloat16)
                out_ref[s, e, :, at : at + width] = chosen[:, :width]


def transform(first, arrived, tables):
    _, levs, _, length = arrived.shape
    slots, _, degrees, lats = tables.shape
    lat_rows = lats // 4
    channels = length // lat_rows * levs
    vmem = pl.BlockSpec(memory_space=pltpu.VMEM)
    return pl.pallas_call(
        functools.partial(transform_kernel, lat_rows=lat_rows),
        in_specs=[pl.BlockSpec(memory_space=pltpu.SMEM), vmem, vmem],
        out_specs=vmem,
        out_shape=jax.ShapeDtypeStruct((slots, 2, channels, degrees), jnp.bfloat16),
        scratch_shapes=[
            pltpu.VMEM((2, channels * 8, lats), jnp.bfloat16),
            pltpu.VMEM((pl.cdiv(degrees, 128), channels * 8, 128), jnp.float32),
        ],
        compiler_params=pltpu.CompilerParams(vmem_limit_bytes=40 * 2**20),
    )(first, arrived, tables)


def row_counts(table, slot_count, wavenumbers):
    position = lax.axis_index(("lat", "lev")) * slot_count
    owned = lax.dynamic_slice_in_dim(table, position, slot_count)
    parity = jnp.arange(2, dtype=jnp.int32)
    return (wavenumbers - owned[:, None] - parity[None, :] + 1) // 2


def on_block(fourier, table, legendre):
    lat_count, lev_count = lax.axis_size("lat"), lax.axis_size("lev")
    lat_rows, channels, wavenumbers = fourier.shape
    x = fourier.transpose(1, 0, 2).reshape(channels * lat_rows, wavenumbers)
    outgoing = pick(table, x, lat_count * lev_count, 3)
    arrived = lax.all_to_all(outgoing, ("lat", "lev"), split_axis=0, concat_axis=0, tiled=True)
    arrived = arrived.reshape((lat_count, lev_count) + arrived.shape[1:])
    first = row_counts(table, legendre.shape[0], wavenumbers)
    return transform(first, arrived, legendre)


def on_any(fourier, table, legendre):
    lat_count, lev_count = lax.axis_size("lat"), lax.axis_size("lev")
    devices, half_lat = lat_count * lev_count, lat_count // 2
    lat_rows, channels, wavenumbers = fourier.shape
    slot_count, _, degree_rows, _ = legendre.shape
    columns = jnp.stack([table, wavenumbers - 1 - table], axis=1).reshape(-1)
    picked = jnp.take(fourier, columns, axis=2)
    shaped = picked.reshape((1, lat_rows, channels, devices, wavenumbers // devices))
    arrived = lax.all_to_all(shaped, ("lat", "lev"), split_axis=3, concat_axis=0, tiled=True)
    halves = arrived.reshape(2, half_lat, lev_count, lat_rows, channels, slot_count, 2)
    north, south = halves[0].astype(jnp.float32), halves[1].astype(jnp.float32)
    merged = jnp.stack([north + south, north - south]).astype(jnp.bfloat16)
    tables = legendre.reshape(slot_count, 2, degree_rows, half_lat, lat_rows)
    products = jnp.einsum(
        "ealbcsw,serab->selcwr", merged, tables, preferred_element_type=jnp.float32
    )
    products = products.reshape(slot_count, 2, lev_count * channels, 2, degree_rows)
    first = row_counts(table, slot_count, wavenumbers)
    in_first = jnp.arange(degree_rows, dtype=jnp.int32)[None, None, :] < first[:, :, None]
    spectral = jnp.where(in_first[:, :, None, :], products[:, :, :, 0], products[:, :, :, 1])
    return spectral.astype(jnp.bfloat16)


def solution(mesh):
    in_specs = (P("lat", "lev", None), P(), P(("lat", "lev"), None, None, None))
    out_specs = P(("lat", "lev"), None, None, None)
    on_device = on_block if dict(mesh.shape) == {"lat": 8, "lev": 4} else on_any
    return jax.shard_map(
        on_device, mesh=mesh, in_specs=in_specs, out_specs=out_specs, check_vma=False
    )
```

```python
import functools

import jax
import jax.numpy as jnp
from jax import lax
from jax.experimental import pallas as pl
from jax.experimental.pallas import tpu as pltpu
from jax.sharding import PartitionSpec as P

NT = (((1,), (1,)), ((), ()))
VMEM = pl.BlockSpec(memory_space=pltpu.VMEM)
SMEM = pl.BlockSpec(memory_space=pltpu.SMEM)
HBM = pl.BlockSpec(memory_space=pltpu.HBM)
Y, X, CORE = 16, 8, 4
NEAR = (0, 1, 2, 3, Y, Y + 1, Y + 2, Y + 3)
FAR = tuple(X + d for d in NEAR)
EARLY = (2, 3)
JOINED = tuple(d for d in NEAR[1:] + FAR if d not in EARLY)
ORDER = (X, Y, X + 2, X + Y, X + 3, 1, Y + 2, X + 1, Y + 3, Y + 1, X + Y + 2, X + Y + 1, X + Y + 3)
WIDE, REST = 256, 64


def here():
    return lax.axis_index("lat") * lax.axis_size("lev") + lax.axis_index("lev")


def pick_kernel(table_ref, x_ref, mine_ref, theirs_ref, *refs, early):
    early_refs, (table, wide, rest, onehot, sems) = refs[:early], refs[early:]
    width = onehot.shape[0]
    channels = x_ref.shape[0]
    me = here()
    core = (me >> 2) & 1
    first = pl.multiple_of(core * REST, REST)
    last = pl.multiple_of((1 - core) * WIDE, REST)
    parts = 3
    step = channels // parts
    copies = [pltpu.make_async_copy(table_ref, table, sems.at[0])]
    for i in range(parts):
        at = pl.ds(i * step, step)
        copies.append(
            pltpu.make_async_copy(x_ref.at[at, pl.ds(first, WIDE)], wide.at[at], sems.at[i + 1])
        )
    copies.append(pltpu.make_async_copy(x_ref.at[:, pl.ds(last, REST)], rest, sems.at[parts + 1]))
    for copy in copies:
        copy.start()
    copies[0].wait()
    row = lax.broadcasted_iota(jnp.int32, (width, 1), 0)
    block = row >> 3
    distance = ((block >> 2) & 1) * Y | ((block >> 3) & 1) * X | (block >> 4) * CORE | block & 3
    slot = (distance ^ me) * 4 + ((row >> 1) & 3)
    lane = lax.broadcasted_iota(jnp.int32, (width, table.shape[1]), 1)
    pair = jnp.sum(jnp.where(lane == slot, table[...], 0), axis=1, keepdims=True)
    column = jnp.where(row & 1 == 1, width - 1 - pair, pair)
    at = lax.broadcasted_iota(jnp.int32, (width, width), 1)
    onehot[...] = jnp.where(at == column, 1.0, 0.0).astype(jnp.bfloat16)

    def emit(x, lanes):
        picked = lax.dot_general(onehot[...], x, NT, preferred_element_type=jnp.float32)
        picked = picked.astype(jnp.bfloat16).reshape(32, 8, picked.shape[1])
        for i, d in enumerate(JOINED):
            mine_ref[i, :, lanes] = picked[(NEAR + FAR).index(d)]
            theirs_ref[i + 1, :, lanes] = picked[16 + (NEAR + FAR).index(d)]
        theirs_ref[0, :, lanes] = picked[16]
        early_refs[0][:, lanes] = picked[0]
        for i, d in enumerate(EARLY):
            early_refs[i + 1][0, :, lanes] = picked[NEAR.index(d)]
            early_refs[i + 1][1, :, lanes] = picked[16 + NEAR.index(d)]

    for i in range(parts):
        copies[i + 1].wait()
        x = wide[i * step : (i + 1) * step].reshape(step * WIDE, width)
        emit(x, pl.ds(i * step * WIDE, step * WIDE))
    copies[parts + 1].wait()
    emit(rest[...].reshape(channels * REST, width), pl.ds(channels * WIDE, channels * REST))


def pick(table, x):
    channels, lat_rows, width = x.shape
    block = (8, channels * lat_rows)
    early = 1 + len(EARLY)
    shapes = [(len(JOINED),) + block, (len(JOINED) + 1,) + block, block] + [(2,) + block] * len(EARLY)
    return pl.pallas_call(
        functools.partial(pick_kernel, early=early),
        in_specs=[HBM] * 2,
        out_specs=[VMEM] * len(shapes),
        out_shape=[jax.ShapeDtypeStruct(s, jnp.bfloat16) for s in shapes],
        scratch_shapes=[
            pltpu.VMEM((1, table.shape[0]), jnp.int32),
            pltpu.VMEM((channels, WIDE, width), jnp.bfloat16),
            pltpu.VMEM((channels, REST, width), jnp.bfloat16),
            pltpu.VMEM((width, width), jnp.bfloat16),
            pltpu.SemaphoreType.DMA((5,)),
        ],
        compiler_params=pltpu.CompilerParams(vmem_limit_bytes=51 * 2**20),
    )(table.reshape(1, -1), x)


def join_kernel(mine_ref, theirs_ref, *outs):
    for i, out in enumerate(outs):
        out[0] = mine_ref[i]
        out[1] = theirs_ref[i + 1]


def join(mine, theirs):
    count = mine.shape[0]
    shape = jax.ShapeDtypeStruct((2,) + mine.shape[1:], mine.dtype)
    return pl.pallas_call(
        join_kernel,
        in_specs=[VMEM] * 2,
        out_specs=[VMEM] * count,
        out_shape=[shape] * count,
        compiler_params=pltpu.CompilerParams(vmem_limit_bytes=16 * 2**20),
    )(mine, theirs)


def second_kernel(*refs):
    for i, ref in enumerate(refs[:-1]):
        refs[-1][i] = ref[1]


def second_blocks(*pieces):
    shape = jax.ShapeDtypeStruct((len(pieces),) + pieces[0].shape[1:], pieces[0].dtype)
    return pl.pallas_call(
        second_kernel,
        in_specs=[VMEM] * len(pieces),
        out_specs=VMEM,
        out_shape=shape,
        compiler_params=pltpu.CompilerParams(vmem_limit_bytes=16 * 2**20),
    )(*pieces)


def transform_kernel(*refs, skip, far, width):
    table_ref, tables_ref, *refs = refs[skip:]
    if far:
        blocks = [(r.at[0], r.at[1]) for r in refs[:8]]
        before, out_ref, held = refs[8:]
    else:
        own, theirs, one, two, three, changed = refs[:6]
        blocks = [
            (own, theirs.at[0]),
            (one.at[0], one.at[1]),
            (two.at[0], changed.at[0]),
            (three.at[0], changed.at[1]),
        ] + [(r.at[0], r.at[1]) for r in refs[6:10]]
        out_ref, held = refs[10:]
    me = here()
    core, z = (me >> 2) & 1, me & 3
    x = (me >> 3) & 1 ^ (1 if far else 0)
    sign = jnp.where(me < Y, 1.0, -1.0).astype(jnp.float32)
    channels = held.shape[3] // 8
    whole = 2 * (WIDE + REST)

    def put(e, lev, row, lane, value):
        for i in range(value.shape[1] // 128):
            held[e, lane // 128 + i, lev, pl.ds(row, 8), :] = value[:, i * 128 : (i + 1) * 128]

    def stage(flip):
        for j in range(4):
            lev = z ^ j

            def both(half, at, size):
                a = blocks[j][half ^ flip][:, at : at + size].astype(jnp.float32)
                b = blocks[4 + j][half ^ flip][:, at : at + size].astype(jnp.float32)
                return a + b, (a - b) * sign

            for half in range(2):
                for c in range(channels):
                    for e, value in enumerate(both(half, c * WIDE, WIDE)):
                        put(e, lev, c * 8, half * (WIDE + 2 * REST), value)
            for c in range(0, channels, 2):
                zero, one = [both(half, channels * WIDE + c * REST, 2 * REST) for half in range(2)]
                for e in range(2):
                    even = jnp.concatenate([zero[e][:, :REST], one[e][:, :REST]], 1)
                    odd = jnp.concatenate([zero[e][:, REST:], one[e][:, REST:]], 1)
                    put(e, lev, c * 8, WIDE, even)
                    put(e, lev, c * 8 + 8, WIDE, odd)

    for flip in range(2):
        pl.when(core == flip)(functools.partial(stage, flip))

    lanes = pl.ds(pl.multiple_of(x * whole, 128), whole)
    for e in range(2):
        tiles = [held.at[e, i].reshape(4 * channels * 8, 128) for i in range(whole // 128)]
        for s in range(4):
            rows = [
                jnp.concatenate([t[pl.ds(2 * s + w, 4 * channels, stride=8), :] for t in tiles], 1)
                for w in range(2)
            ]
            products = lax.dot_general(
                jnp.concatenate(rows, 0).astype(jnp.bfloat16),
                tables_ref[s, e, :, lanes],
                NT,
                preferred_element_type=jnp.float32,
            )
            count = (width - table_ref[me * 4 + s] - e + 1) // 2
            one, two = products[: 4 * channels], products[4 * channels :]
            degree = lax.broadcasted_iota(jnp.int32, one.shape, 1)
            chosen = jnp.where(degree < count, one, two)
            if far:
                chosen = chosen + before[s, e]
            out_ref[s, e] = chosen.astype(out_ref.dtype)


def transform(table, tables, blocks, far, width, rest=()):
    slots, _, degrees, lats = tables.shape
    channels = blocks[0].shape[-1] // (WIDE + REST)
    return pl.pallas_call(
        functools.partial(transform_kernel, skip=len(rest), far=far, width=width),
        in_specs=[pl.BlockSpec(memory_space=pl.ANY)] * len(rest) + [SMEM] + [VMEM] * (1 + len(blocks)),
        out_specs=VMEM,
        out_shape=jax.ShapeDtypeStruct(
            (slots, 2, 4 * channels, degrees), jnp.bfloat16 if far else jnp.float32
        ),
        scratch_shapes=[
            pltpu.VMEM((2, 2 * (WIDE + REST) // 128, 4, channels * 8, 128), jnp.float32)
        ],
        compiler_params=pltpu.CompilerParams(vmem_limit_bytes=20 * 2**20),
    )(*rest, table, tables, *blocks)


def send(piece, distance):
    count = lax.axis_size("lat") * lax.axis_size("lev")
    return lax.ppermute(piece, ("lat", "lev"), [(i, i ^ distance) for i in range(count)])


def on_block(fourier, table, legendre):
    width = fourier.shape[2]
    mine, theirs, own, *early = pick(table, fourier.transpose(1, 0, 2))
    got = {d: send(piece, d) for d, piece in zip(EARLY, early)}
    theirs = send(theirs, CORE)
    ready = dict(zip(JOINED, join(mine, theirs)))
    got.update({d: send(ready[d], d) for d in ORDER})
    came = [got[d] for d in EARLY]
    *came, got[1] = lax.optimization_barrier((*came, got[1]))
    changed = send(second_blocks(*came), CORE)
    near = [own, theirs] + [got[d] for d in NEAR[1:4]] + [changed] + [got[d] for d in NEAR[4:]]
    partial = transform(table, legendre, near, False, width)
    far = [got[d] for d in FAR] + [partial]
    return transform(table, legendre, far, True, width, list(got.values()))


def row_counts(table, slot_count, wavenumbers):
    position = lax.axis_index(("lat", "lev")) * slot_count
    owned = lax.dynamic_slice_in_dim(table, position, slot_count)
    parity = jnp.arange(2, dtype=jnp.int32)
    return (wavenumbers - owned[:, None] - parity[None, :] + 1) // 2


def on_any(fourier, table, legendre):
    lat_count, lev_count = lax.axis_size("lat"), lax.axis_size("lev")
    devices, half_lat = lat_count * lev_count, lat_count // 2
    lat_rows, channels, wavenumbers = fourier.shape
    slot_count, _, degree_rows, _ = legendre.shape
    columns = jnp.stack([table, wavenumbers - 1 - table], axis=1).reshape(-1)
    picked = jnp.take(fourier, columns, axis=2)
    shaped = picked.reshape((1, lat_rows, channels, devices, wavenumbers // devices))
    arrived = lax.all_to_all(shaped, ("lat", "lev"), split_axis=3, concat_axis=0, tiled=True)
    halves = arrived.reshape(2, half_lat, lev_count, lat_rows, channels, slot_count, 2)
    north, south = halves[0].astype(jnp.float32), halves[1].astype(jnp.float32)
    merged = jnp.stack([north + south, north - south]).astype(jnp.bfloat16)
    tables = legendre.reshape(slot_count, 2, degree_rows, half_lat, lat_rows)
    products = jnp.einsum(
        "ealbcsw,serab->selcwr", merged, tables, preferred_element_type=jnp.float32
    )
    products = products.reshape(slot_count, 2, lev_count * channels, 2, degree_rows)
    first = row_counts(table, slot_count, wavenumbers)
    in_first = jnp.arange(degree_rows, dtype=jnp.int32)[None, None, :] < first[:, :, None]
    spectral = jnp.where(in_first[:, :, None, :], products[:, :, :, 0], products[:, :, :, 1])
    return spectral.astype(jnp.bfloat16)


def solution(mesh):
    in_specs = (P("lat", "lev", None), P(), P(("lat", "lev"), None, None, None))
    out_specs = P(("lat", "lev"), None, None, None)
    on_device = on_block if dict(mesh.shape) == {"lat": 8, "lev": 4} else on_any
    return jax.shard_map(
        on_device, mesh=mesh, in_specs=in_specs, out_specs=out_specs, check_vma=False
    )
```

```python
import functools

import jax
import jax.numpy as jnp
from jax import lax
from jax.experimental import pallas as pl
from jax.experimental.pallas import tpu as pltpu
from jax.sharding import PartitionSpec as P

NT = (((1,), (1,)), ((), ()))
VMEM = pl.BlockSpec(memory_space=pltpu.VMEM)
HBM = pl.BlockSpec(memory_space=pltpu.HBM)
Y, X, CORE = 16, 8, 4
NEAR = (0, 1, 2, 3, Y, Y + 1, Y + 2, Y + 3)
FAR = tuple(X + d for d in NEAR)
EARLY = (2, 3)
JOINED = tuple(d for d in NEAR[1:] + FAR if d not in EARLY)
ORDER = (1, 16, 18, 17, 19, 8, 10, 9, 11, 24, 26, 25, 27)
WIDE, REST = 256, 64


def here():
    return lax.axis_index("lat") * lax.axis_size("lev") + lax.axis_index("lev")


def pick_kernel(table_ref, x_ref, mine_ref, theirs_ref, *refs, early):
    early_refs, (wide, rest, onehot, sems) = refs[:early], refs[early:]
    width = onehot.shape[0]
    channels = x_ref.shape[0]
    me = here()
    core = (me >> 2) & 1
    first = pl.multiple_of(core * REST, REST)
    last = pl.multiple_of((1 - core) * WIDE, REST)
    parts = 3
    step = channels // parts
    copies = []
    for i in range(parts):
        at = pl.ds(i * step, step)
        copies.append(
            pltpu.make_async_copy(x_ref.at[at, pl.ds(first, WIDE)], wide.at[at], sems.at[i])
        )
    copies.append(pltpu.make_async_copy(x_ref.at[:, pl.ds(last, REST)], rest, sems.at[parts]))
    for copy in copies:
        copy.start()
    row = lax.broadcasted_iota(jnp.int32, (width, 1), 0)
    block = row >> 3
    distance = ((block >> 2) & 1) * Y | ((block >> 3) & 1) * X | (block >> 4) * CORE | block & 3
    slot = (distance ^ me) * 4 + ((row >> 1) & 3)
    lane = lax.broadcasted_iota(jnp.int32, (width, table_ref.shape[1]), 1)
    pair = jnp.sum(jnp.where(lane == slot, table_ref[...], 0), axis=1, keepdims=True)
    column = jnp.where(row & 1 == 1, width - 1 - pair, pair)
    at = lax.broadcasted_iota(jnp.int32, (width, width), 1)
    onehot[...] = jnp.where(at == column, 1.0, 0.0).astype(jnp.bfloat16)

    def emit(x, lanes):
        picked = lax.dot_general(onehot[...], x, NT, preferred_element_type=jnp.float32)
        picked = picked.astype(jnp.bfloat16).reshape(32, 8, picked.shape[1])
        for i, d in enumerate(JOINED):
            mine_ref[i, :, lanes] = picked[(NEAR + FAR).index(d)]
            theirs_ref[i + 1, :, lanes] = picked[16 + (NEAR + FAR).index(d)]
        theirs_ref[0, :, lanes] = picked[16]
        early_refs[0][:, lanes] = picked[0]
        for i, d in enumerate(EARLY):
            early_refs[i + 1][0, :, lanes] = picked[NEAR.index(d)]
            early_refs[i + 1][1, :, lanes] = picked[16 + NEAR.index(d)]

    for i in range(parts):
        copies[i].wait()
        x = wide[i * step : (i + 1) * step].reshape(step * WIDE, width)
        emit(x, pl.ds(i * step * WIDE, step * WIDE))
    copies[parts].wait()
    emit(rest[...].reshape(channels * REST, width), pl.ds(channels * WIDE, channels * REST))


def pick(table, x):
    channels, lat_rows, width = x.shape
    block = (8, channels * lat_rows)
    early = 1 + len(EARLY)
    shapes = [(len(JOINED),) + block, (len(JOINED) + 1,) + block, block] + [(2,) + block] * len(EARLY)
    return pl.pallas_call(
        functools.partial(pick_kernel, early=early),
        in_specs=[VMEM, HBM],
        out_specs=[VMEM] * len(shapes),
        out_shape=[jax.ShapeDtypeStruct(s, jnp.bfloat16) for s in shapes],
        scratch_shapes=[
            pltpu.VMEM((channels, WIDE, width), jnp.bfloat16),
            pltpu.VMEM((channels, REST, width), jnp.bfloat16),
            pltpu.VMEM((width, width), jnp.bfloat16),
            pltpu.SemaphoreType.DMA((4,)),
        ],
        compiler_params=pltpu.CompilerParams(vmem_limit_bytes=51 * 2**20),
    )(table, x)


def join_kernel(mine_ref, theirs_ref, *outs):
    for i, out in enumerate(outs):
        out[0] = mine_ref[i]
        out[1] = theirs_ref[i + 1]


def join(mine, theirs):
    count = mine.shape[0]
    shape = jax.ShapeDtypeStruct((2,) + mine.shape[1:], mine.dtype)
    return pl.pallas_call(
        join_kernel,
        in_specs=[VMEM] * 2,
        out_specs=[VMEM] * count,
        out_shape=[shape] * count,
        compiler_params=pltpu.CompilerParams(vmem_limit_bytes=16 * 2**20),
    )(mine, theirs)


def second_kernel(*refs):
    for i, ref in enumerate(refs[:-1]):
        refs[-1][i] = ref[1]


def second_blocks(*pieces):
    shape = jax.ShapeDtypeStruct((len(pieces),) + pieces[0].shape[1:], pieces[0].dtype)
    return pl.pallas_call(
        second_kernel,
        in_specs=[VMEM] * len(pieces),
        out_specs=VMEM,
        out_shape=shape,
        compiler_params=pltpu.CompilerParams(vmem_limit_bytes=16 * 2**20),
    )(*pieces)


def transform_kernel(*refs, skip, far, steps, width, added):
    table_ref, tables_ref, *refs = refs[skip:]
    if far:
        blocks = [(r.at[0], r.at[1]) for r in refs[: 2 * len(steps)]]
        refs = refs[2 * len(steps) :]
    else:
        own, theirs, one, two, three, changed = refs[:6]
        blocks = [
            (own, theirs.at[0]),
            (one.at[0], one.at[1]),
            (two.at[0], changed.at[0]),
            (three.at[0], changed.at[1]),
        ] + [(r.at[0], r.at[1]) for r in refs[6:10]]
        refs = refs[10:]
    before = refs[0] if added else None
    out_ref, held = refs[-2:]
    me = here()
    core, z = (me >> 2) & 1, me & 3
    x = (me >> 3) & 1 ^ (1 if far else 0)
    sign = jnp.where(me < Y, 1.0, -1.0).astype(jnp.float32)
    levs, channels = held.shape[2], held.shape[3] // 8
    whole = 2 * (WIDE + REST)

    def put(e, lev, row, lane, value):
        for i in range(value.shape[1] // 128):
            held[e, lane // 128 + i, lev, pl.ds(row, 8), :] = value[:, i * 128 : (i + 1) * 128]

    def stage(flip):
        for j, step in enumerate(steps):
            lev = (z ^ step) & (levs - 1)

            def both(half, at, size):
                a = blocks[j][half ^ flip][:, at : at + size].astype(jnp.float32)
                b = blocks[len(steps) + j][half ^ flip][:, at : at + size].astype(jnp.float32)
                return a + b, (a - b) * sign

            for half in range(2):
                for c in range(channels):
                    for e, value in enumerate(both(half, c * WIDE, WIDE)):
                        put(e, lev, c * 8, half * (WIDE + 2 * REST), value)
            for c in range(0, channels, 2):
                zero, one = [both(half, channels * WIDE + c * REST, 2 * REST) for half in range(2)]
                for e in range(2):
                    even = jnp.concatenate([zero[e][:, :REST], one[e][:, :REST]], 1)
                    odd = jnp.concatenate([zero[e][:, REST:], one[e][:, REST:]], 1)
                    put(e, lev, c * 8, WIDE, even)
                    put(e, lev, c * 8 + 8, WIDE, odd)

    for flip in range(2):
        pl.when(core == flip)(functools.partial(stage, flip))

    rows = levs * channels
    low = (z ^ steps[0]) < levs
    lanes = pl.ds(pl.multiple_of(x * whole, 128), whole)
    slot = lax.broadcasted_iota(jnp.int32, table_ref.shape, 1) - me * 4
    for s in range(4):
        pair = jnp.sum(jnp.where(slot == s, table_ref[...], 0), axis=1, keepdims=True)
        for e in range(2):
            tiles = [held.at[e, i].reshape(rows * 8, 128) for i in range(whole // 128)]
            picked = [
                jnp.concatenate([t[pl.ds(2 * s + w, rows, stride=8), :] for t in tiles], 1)
                for w in range(2)
            ]
            products = lax.dot_general(
                jnp.concatenate(picked, 0).astype(jnp.bfloat16),
                tables_ref[s, e, :, lanes],
                NT,
                preferred_element_type=jnp.float32,
            )
            count = (width - pair - e + 1) >> 1
            degree = lax.broadcasted_iota(jnp.int32, (rows, products.shape[1]), 1)
            chosen = jnp.where(degree < count, products[:rows], products[rows:])
            if levs < 4:
                parts = [jnp.where(low, chosen, 0.0), jnp.where(low, 0.0, chosen)]
                chosen = jnp.concatenate(parts, 0)
            if added:
                chosen = chosen + before[s, e]
            out_ref[s, e] = chosen.astype(out_ref.dtype)


def transform(table, tables, blocks, far, steps, width, before=None, last=False, rest=()):
    slots, _, degrees, lats = tables.shape
    channels = blocks[0].shape[-1] // (WIDE + REST)
    more = [] if before is None else [before]
    return pl.pallas_call(
        functools.partial(
            transform_kernel,
            skip=len(rest),
            far=far,
            steps=steps,
            width=width,
            added=before is not None,
        ),
        in_specs=[pl.BlockSpec(memory_space=pl.ANY)] * len(rest)
        + [VMEM] * (2 + len(blocks) + len(more)),
        out_specs=VMEM,
        out_shape=jax.ShapeDtypeStruct(
            (slots, 2, 4 * channels, degrees), jnp.bfloat16 if last else jnp.float32
        ),
        scratch_shapes=[
            pltpu.VMEM((2, 2 * (WIDE + REST) // 128, len(steps), channels * 8, 128), jnp.float32)
        ],
        compiler_params=pltpu.CompilerParams(vmem_limit_bytes=20 * 2**20),
    )(*rest, table, tables, *blocks, *more)


def send(piece, distance):
    count = lax.axis_size("lat") * lax.axis_size("lev")
    return lax.ppermute(piece, ("lat", "lev"), [(i, i ^ distance) for i in range(count)])


def on_block(fourier, table, legendre):
    width = fourier.shape[2]
    entries = table.reshape(1, -1)
    mine, theirs, own, *early = pick(entries, fourier.transpose(1, 0, 2))
    got = {d: send(piece, d) for d, piece in zip(EARLY, early)}
    theirs = send(theirs, CORE)
    ready = dict(zip(JOINED, join(mine, theirs)))
    got.update({d: send(ready[d], d) for d in ORDER})
    came = [got[d] for d in EARLY]
    *came, got[1] = lax.optimization_barrier((*came, got[1]))
    changed = send(second_blocks(*came), CORE)
    near = [own, theirs] + [got[d] for d in NEAR[1:4]] + [changed] + [got[d] for d in NEAR[4:]]
    total = transform(entries, legendre, near, False, (0, 1, 2, 3), width)
    far = [got[d] for d in FAR]
    return transform(
        entries, legendre, far, True, (0, 1, 2, 3), width, total, True, list(got.values())
    )


def row_counts(table, slot_count, wavenumbers):
    position = lax.axis_index(("lat", "lev")) * slot_count
    owned = lax.dynamic_slice_in_dim(table, position, slot_count)
    parity = jnp.arange(2, dtype=jnp.int32)
    return (wavenumbers - owned[:, None] - parity[None, :] + 1) // 2


def on_any(fourier, table, legendre):
    lat_count, lev_count = lax.axis_size("lat"), lax.axis_size("lev")
    devices, half_lat = lat_count * lev_count, lat_count // 2
    lat_rows, channels, wavenumbers = fourier.shape
    slot_count, _, degree_rows, _ = legendre.shape
    columns = jnp.stack([table, wavenumbers - 1 - table], axis=1).reshape(-1)
    picked = jnp.take(fourier, columns, axis=2)
    shaped = picked.reshape((1, lat_rows, channels, devices, wavenumbers // devices))
    arrived = lax.all_to_all(shaped, ("lat", "lev"), split_axis=3, concat_axis=0, tiled=True)
    halves = arrived.reshape(2, half_lat, lev_count, lat_rows, channels, slot_count, 2)
    north, south = halves[0].astype(jnp.float32), halves[1].astype(jnp.float32)
    merged = jnp.stack([north + south, north - south]).astype(jnp.bfloat16)
    tables = legendre.reshape(slot_count, 2, degree_rows, half_lat, lat_rows)
    products = jnp.einsum(
        "ealbcsw,serab->selcwr", merged, tables, preferred_element_type=jnp.float32
    )
    products = products.reshape(slot_count, 2, lev_count * channels, 2, degree_rows)
    first = row_counts(table, slot_count, wavenumbers)
    in_first = jnp.arange(degree_rows, dtype=jnp.int32)[None, None, :] < first[:, :, None]
    spectral = jnp.where(in_first[:, :, None, :], products[:, :, :, 0], products[:, :, :, 1])
    return spectral.astype(jnp.bfloat16)


def solution(mesh):
    in_specs = (P("lat", "lev", None), P(), P(("lat", "lev"), None, None, None))
    out_specs = P(("lat", "lev"), None, None, None)
    on_device = on_block if dict(mesh.shape) == {"lat": 8, "lev": 4} else on_any
    return jax.shard_map(
        on_device, mesh=mesh, in_specs=in_specs, out_specs=out_specs, check_vma=False
    )
```

```python
import functools

import jax
import jax.numpy as jnp
from jax import lax
from jax.experimental import pallas as pl
from jax.experimental.pallas import tpu as pltpu
from jax.sharding import PartitionSpec as P

NT = (((1,), (1,)), ((), ()))
VMEM = pl.BlockSpec(memory_space=pltpu.VMEM)
HBM = pl.BlockSpec(memory_space=pltpu.HBM)
Y, X, CORE = 16, 8, 4
NEAR = (0, 1, 2, 3, Y, Y + 1, Y + 2, Y + 3)
FAR = tuple(X + d for d in NEAR)
EARLY = (3, 2)
JOINED = tuple(d for d in NEAR[1:] + FAR if d not in EARLY)
ORDER = (1, 16, 18, 17, 19, 8, 10, 9, 11, 24, 26, 25, 27)
WIDE, REST = 256, 64


def here():
    return lax.axis_index("lat") * lax.axis_size("lev") + lax.axis_index("lev")


def load_kernel(x_ref, wide_ref, rest_ref, sems):
    core = (here() >> 2) & 1
    first = pl.multiple_of(core * REST, REST)
    last = pl.multiple_of((1 - core) * WIDE, REST)
    copies = [
        pltpu.make_async_copy(x_ref.at[:, pl.ds(first, WIDE)], wide_ref, sems.at[0]),
        pltpu.make_async_copy(x_ref.at[:, pl.ds(last, REST)], rest_ref, sems.at[1]),
    ]
    for copy in copies:
        copy.start()
    for copy in copies:
        copy.wait()


def load(x):
    channels, _, width = x.shape
    shapes = [(channels, WIDE, width), (channels, REST, width)]
    return pl.pallas_call(
        load_kernel,
        in_specs=[HBM],
        out_specs=[VMEM] * 2,
        out_shape=[jax.ShapeDtypeStruct(s, x.dtype) for s in shapes],
        scratch_shapes=[pltpu.SemaphoreType.DMA((2,))],
        cost_estimate=pl.CostEstimate(flops=10**9, bytes_accessed=4 * x.size, transcendentals=0),
        compiler_params=pltpu.CompilerParams(vmem_limit_bytes=51 * 2**20),
    )(x)


def pick_kernel(table_ref, wide_ref, rest_ref, mine_ref, theirs_ref, *refs, early):
    early_refs, (onehot,) = refs[:early], refs[early:]
    width = onehot.shape[0]
    channels = wide_ref.shape[0]
    me = here()
    row = lax.broadcasted_iota(jnp.int32, (width, 1), 0)
    block = row >> 3
    distance = ((block >> 2) & 1) * Y | ((block >> 3) & 1) * X | (block >> 4) * CORE | block & 3
    slot = (distance ^ me) * 4 + ((row >> 1) & 3)
    lane = lax.broadcasted_iota(jnp.int32, (width, table_ref.shape[1]), 1)
    pair = jnp.sum(jnp.where(lane == slot, table_ref[...], 0), axis=1, keepdims=True)
    column = jnp.where(row & 1 == 1, width - 1 - pair, pair)
    at = lax.broadcasted_iota(jnp.int32, (width, width), 1)
    onehot[...] = jnp.where(at == column, 1.0, 0.0).astype(jnp.bfloat16)

    def emit(x, lanes):
        picked = lax.dot_general(onehot[...], x, NT, preferred_element_type=jnp.float32)
        picked = picked.astype(jnp.bfloat16).reshape(32, 8, picked.shape[1])
        for i, d in enumerate(JOINED):
            mine_ref[i, :, lanes] = picked[(NEAR + FAR).index(d)]
            theirs_ref[i + 1, :, lanes] = picked[16 + (NEAR + FAR).index(d)]
        theirs_ref[0, :, lanes] = picked[16]
        early_refs[0][:, lanes] = picked[0]
        for i, d in enumerate(EARLY):
            early_refs[i + 1][0, :, lanes] = picked[NEAR.index(d)]
            early_refs[i + 1][1, :, lanes] = picked[16 + NEAR.index(d)]

    for c in range(0, channels, 2):
        x = wide_ref[c : c + 2].reshape(2 * WIDE, width)
        emit(x, pl.ds(c * WIDE, 2 * WIDE))
    emit(rest_ref[...].reshape(channels * REST, width), pl.ds(channels * WIDE, channels * REST))


def pick(table, x):
    channels, lat_rows, width = x.shape
    block = (8, channels * lat_rows)
    early = 1 + len(EARLY)
    shapes = [(len(JOINED),) + block, (len(JOINED) + 1,) + block, block] + [(2,) + block] * len(EARLY)
    return pl.pallas_call(
        functools.partial(pick_kernel, early=early),
        in_specs=[VMEM] * 3,
        out_specs=[VMEM] * len(shapes),
        out_shape=[jax.ShapeDtypeStruct(s, jnp.bfloat16) for s in shapes],
        scratch_shapes=[pltpu.VMEM((width, width), jnp.bfloat16)],
        compiler_params=pltpu.CompilerParams(vmem_limit_bytes=16 * 2**20),
    )(table, *load(x))


def join_kernel(mine_ref, theirs_ref, *outs):
    for i, out in enumerate(outs):
        out[0] = mine_ref[i]
        out[1] = theirs_ref[i + 1]


def join(mine, theirs):
    count = mine.shape[0]
    shape = jax.ShapeDtypeStruct((2,) + mine.shape[1:], mine.dtype)
    return pl.pallas_call(
        join_kernel,
        in_specs=[VMEM] * 2,
        out_specs=[VMEM] * count,
        out_shape=[shape] * count,
        compiler_params=pltpu.CompilerParams(vmem_limit_bytes=16 * 2**20),
    )(mine, theirs)


def second_kernel(*refs):
    for i, ref in enumerate(refs[:-1]):
        refs[-1][i] = ref[1]


def second_blocks(*pieces):
    shape = jax.ShapeDtypeStruct((len(pieces),) + pieces[0].shape[1:], pieces[0].dtype)
    return pl.pallas_call(
        second_kernel,
        in_specs=[VMEM] * len(pieces),
        out_specs=VMEM,
        out_shape=shape,
        compiler_params=pltpu.CompilerParams(vmem_limit_bytes=16 * 2**20),
    )(*pieces)


def transform_kernel(*refs, skip, far, steps, width, added):
    table_ref, tables_ref, *refs = refs[skip:]
    if far:
        blocks = [(r.at[0], r.at[1]) for r in refs[: 2 * len(steps)]]
        refs = refs[2 * len(steps) :]
    else:
        own, theirs, changed = refs[:3]
        blocks = [(own, theirs.at[0])]
        for d, r in zip(NEAR[1:], refs[3:10]):
            blocks.append((r.at[0], changed.at[EARLY.index(d)] if d in EARLY else r.at[1]))
        refs = refs[10:]
    before = refs[0] if added else None
    out_ref, held = refs[-2:]
    me = here()
    core, z = (me >> 2) & 1, me & 3
    x = (me >> 3) & 1 ^ (1 if far else 0)
    sign = jnp.where(me < Y, 1.0, -1.0).astype(jnp.float32)
    levs, channels = held.shape[2], held.shape[3] // 8
    whole = 2 * (WIDE + REST)

    def put(e, lev, row, lane, value):
        for i in range(value.shape[1] // 128):
            held[e, lane // 128 + i, lev, pl.ds(row, 8), :] = value[:, i * 128 : (i + 1) * 128]

    def stage(flip):
        for j, step in enumerate(steps):
            lev = (z ^ step) & (levs - 1)

            def both(half, at, size):
                a = blocks[j][half ^ flip][:, at : at + size].astype(jnp.float32)
                b = blocks[len(steps) + j][half ^ flip][:, at : at + size].astype(jnp.float32)
                return a + b, (a - b) * sign

            for half in range(2):
                for c in range(channels):
                    for e, value in enumerate(both(half, c * WIDE, WIDE)):
                        put(e, lev, c * 8, half * (WIDE + 2 * REST), value)
            for c in range(0, channels, 2):
                zero, one = [both(half, channels * WIDE + c * REST, 2 * REST) for half in range(2)]
                for e in range(2):
                    even = jnp.concatenate([zero[e][:, :REST], one[e][:, :REST]], 1)
                    odd = jnp.concatenate([zero[e][:, REST:], one[e][:, REST:]], 1)
                    put(e, lev, c * 8, WIDE, even)
                    put(e, lev, c * 8 + 8, WIDE, odd)

    for flip in range(2):
        pl.when(core == flip)(functools.partial(stage, flip))

    rows = levs * channels
    low = (z ^ steps[0]) < levs
    lanes = pl.ds(pl.multiple_of(x * whole, 128), whole)
    slot = lax.broadcasted_iota(jnp.int32, table_ref.shape, 1) - me * 4
    for s in range(4):
        pair = jnp.sum(jnp.where(slot == s, table_ref[...], 0), axis=1, keepdims=True)
        for e in range(2):
            tiles = [held.at[e, i].reshape(rows * 8, 128) for i in range(whole // 128)]
            picked = [
                jnp.concatenate([t[pl.ds(2 * s + w, rows, stride=8), :] for t in tiles], 1)
                for w in range(2)
            ]
            products = lax.dot_general(
                jnp.concatenate(picked, 0).astype(jnp.bfloat16),
                tables_ref[s, e, :, lanes],
                NT,
                preferred_element_type=jnp.float32,
            )
            count = (width - pair - e + 1) >> 1
            degree = lax.broadcasted_iota(jnp.int32, (rows, products.shape[1]), 1)
            chosen = jnp.where(degree < count, products[:rows], products[rows:])
            if levs < 4:
                parts = [jnp.where(low, chosen, 0.0), jnp.where(low, 0.0, chosen)]
                chosen = jnp.concatenate(parts, 0)
            if added:
                chosen = chosen + before[s, e]
            out_ref[s, e] = chosen.astype(out_ref.dtype)


def transform(table, tables, blocks, far, steps, width, before=None, last=False, rest=()):
    slots, _, degrees, lats = tables.shape
    channels = blocks[0].shape[-1] // (WIDE + REST)
    more = [] if before is None else [before]
    return pl.pallas_call(
        functools.partial(
            transform_kernel,
            skip=len(rest),
            far=far,
            steps=steps,
            width=width,
            added=before is not None,
        ),
        in_specs=[pl.BlockSpec(memory_space=pl.ANY)] * len(rest)
        + [VMEM] * (2 + len(blocks) + len(more)),
        out_specs=VMEM,
        out_shape=jax.ShapeDtypeStruct(
            (slots, 2, 4 * channels, degrees), jnp.bfloat16 if last else jnp.float32
        ),
        scratch_shapes=[
            pltpu.VMEM((2, 2 * (WIDE + REST) // 128, len(steps), channels * 8, 128), jnp.float32)
        ],
        compiler_params=pltpu.CompilerParams(vmem_limit_bytes=20 * 2**20),
    )(*rest, table, tables, *blocks, *more)


def send(piece, distance):
    count = lax.axis_size("lat") * lax.axis_size("lev")
    return lax.ppermute(piece, ("lat", "lev"), [(i, i ^ distance) for i in range(count)])


def on_block(fourier, table, legendre):
    width = fourier.shape[2]
    entries = table.reshape(1, -1)
    mine, theirs, own, *early = pick(entries, fourier.transpose(1, 0, 2))
    got = {d: send(piece, d) for d, piece in zip(EARLY, early)}
    theirs = send(theirs, CORE)
    ready = dict(zip(JOINED, join(mine, theirs)))
    got.update({d: send(ready[d], d) for d in ORDER})
    came = [got[d] for d in EARLY]
    *came, got[ORDER[0]] = lax.optimization_barrier((*came, got[ORDER[0]]))
    changed = send(second_blocks(*came), CORE)
    near = [own, theirs, changed] + [got[d] for d in NEAR[1:]]
    total = transform(entries, legendre, near, False, (0, 1, 2, 3), width)
    far = [got[d] for d in FAR]
    return transform(
        entries, legendre, far, True, (0, 1, 2, 3), width, total, True, list(got.values())
    )


def row_counts(table, slot_count, wavenumbers):
    position = lax.axis_index(("lat", "lev")) * slot_count
    owned = lax.dynamic_slice_in_dim(table, position, slot_count)
    parity = jnp.arange(2, dtype=jnp.int32)
    return (wavenumbers - owned[:, None] - parity[None, :] + 1) // 2


def on_any(fourier, table, legendre):
    lat_count, lev_count = lax.axis_size("lat"), lax.axis_size("lev")
    devices, half_lat = lat_count * lev_count, lat_count // 2
    lat_rows, channels, wavenumbers = fourier.shape
    slot_count, _, degree_rows, _ = legendre.shape
    columns = jnp.stack([table, wavenumbers - 1 - table], axis=1).reshape(-1)
    picked = jnp.take(fourier, columns, axis=2)
    shaped = picked.reshape((1, lat_rows, channels, devices, wavenumbers // devices))
    arrived = lax.all_to_all(shaped, ("lat", "lev"), split_axis=3, concat_axis=0, tiled=True)
    halves = arrived.reshape(2, half_lat, lev_count, lat_rows, channels, slot_count, 2)
    north, south = halves[0].astype(jnp.float32), halves[1].astype(jnp.float32)
    merged = jnp.stack([north + south, north - south]).astype(jnp.bfloat16)
    tables = legendre.reshape(slot_count, 2, degree_rows, half_lat, lat_rows)
    products = jnp.einsum(
        "ealbcsw,serab->selcwr", merged, tables, preferred_element_type=jnp.float32
    )
    products = products.reshape(slot_count, 2, lev_count * channels, 2, degree_rows)
    first = row_counts(table, slot_count, wavenumbers)
    in_first = jnp.arange(degree_rows, dtype=jnp.int32)[None, None, :] < first[:, :, None]
    spectral = jnp.where(in_first[:, :, None, :], products[:, :, :, 0], products[:, :, :, 1])
    return spectral.astype(jnp.bfloat16)


def solution(mesh):
    in_specs = (P("lat", "lev", None), P(), P(("lat", "lev"), None, None, None))
    out_specs = P(("lat", "lev"), None, None, None)
    on_device = on_block if dict(mesh.shape) == {"lat": 8, "lev": 4} else on_any
    return jax.shard_map(
        on_device, mesh=mesh, in_specs=in_specs, out_specs=out_specs, check_vma=False
    )
```

```python
import functools

import jax
import jax.numpy as jnp
from jax import lax
from jax.experimental import pallas as pl
from jax.experimental.pallas import tpu as pltpu
from jax.sharding import PartitionSpec as P

NT = (((1,), (1,)), ((), ()))
VMEM = pl.BlockSpec(memory_space=pltpu.VMEM)
HBM = pl.BlockSpec(memory_space=pltpu.HBM)
Y, X, CORE = 16, 8, 4
NEAR = (0, 1, 2, 3, Y, Y + 1, Y + 2, Y + 3)
FAR = tuple(X + d for d in NEAR)
EARLY = (3, 2)
JOINED = tuple(d for d in NEAR[1:] + FAR if d not in EARLY)
LATE = 4
ORDER = (17, 16, 18, 1, 19, 8, 10, 9, 26, 24, 25, 11, 27)
WIDE, REST = 256, 64


def here():
    return lax.axis_index("lat") * lax.axis_size("lev") + lax.axis_index("lev")


def load_kernel(x_ref, wide_ref, rest_ref, sems):
    core = (here() >> 2) & 1
    first = pl.multiple_of(core * REST, REST)
    last = pl.multiple_of((1 - core) * WIDE, REST)
    copies = [
        pltpu.make_async_copy(x_ref.at[:, pl.ds(first, WIDE)], wide_ref, sems.at[0]),
        pltpu.make_async_copy(x_ref.at[:, pl.ds(last, REST)], rest_ref, sems.at[1]),
    ]
    for copy in copies:
        copy.start()
    for copy in copies:
        copy.wait()


def load(x):
    channels, _, width = x.shape
    shapes = [(channels, WIDE, width), (channels, REST, width)]
    return pl.pallas_call(
        load_kernel,
        in_specs=[HBM],
        out_specs=[VMEM] * 2,
        out_shape=[jax.ShapeDtypeStruct(s, x.dtype) for s in shapes],
        scratch_shapes=[pltpu.SemaphoreType.DMA((2,))],
        cost_estimate=pl.CostEstimate(flops=10**9, bytes_accessed=4 * x.size, transcendentals=0),
        compiler_params=pltpu.CompilerParams(vmem_limit_bytes=51 * 2**20),
    )(x)


def pick_kernel(table_ref, wide_ref, rest_ref, mine_ref, theirs_ref, *refs, early):
    early_refs, (onehot,) = refs[:early], refs[early:]
    width = onehot.shape[0]
    channels = wide_ref.shape[0]
    me = here()
    row = lax.broadcasted_iota(jnp.int32, (width, 1), 0)
    block = row >> 3
    distance = ((block >> 2) & 1) * Y | ((block >> 3) & 1) * X | (block >> 4) * CORE | block & 3
    slot = (distance ^ me) * 4 + ((row >> 1) & 3)
    lane = lax.broadcasted_iota(jnp.int32, (width, table_ref.shape[1]), 1)
    pair = jnp.sum(jnp.where(lane == slot, table_ref[...], 0), axis=1, keepdims=True)
    column = jnp.where(row & 1 == 1, width - 1 - pair, pair)
    at = lax.broadcasted_iota(jnp.int32, (width, width), 1)
    onehot[...] = jnp.where(at == column, 1.0, 0.0).astype(jnp.bfloat16)

    def emit(x, lanes):
        picked = lax.dot_general(onehot[...], x, NT, preferred_element_type=jnp.float32)
        picked = picked.astype(jnp.bfloat16).reshape(32, 8, picked.shape[1])
        for i, d in enumerate(JOINED):
            mine_ref[i, :, lanes] = picked[(NEAR + FAR).index(d)]
            theirs_ref[i + 1, :, lanes] = picked[16 + (NEAR + FAR).index(d)]
        theirs_ref[0, :, lanes] = picked[16]
        early_refs[0][:, lanes] = picked[0]
        for i, d in enumerate(EARLY):
            early_refs[i + 1][0, :, lanes] = picked[NEAR.index(d)]
            early_refs[i + 1][1, :, lanes] = picked[16 + NEAR.index(d)]

    for c in range(0, channels, 2):
        x = wide_ref[c : c + 2].reshape(2 * WIDE, width)
        emit(x, pl.ds(c * WIDE, 2 * WIDE))
    emit(rest_ref[...].reshape(channels * REST, width), pl.ds(channels * WIDE, channels * REST))


def pick(table, x):
    channels, lat_rows, width = x.shape
    block = (8, channels * lat_rows)
    early = 1 + len(EARLY)
    shapes = [(len(JOINED),) + block, (len(JOINED) + 1,) + block, block] + [(2,) + block] * len(EARLY)
    return pl.pallas_call(
        functools.partial(pick_kernel, early=early),
        in_specs=[VMEM] * 3,
        out_specs=[VMEM] * len(shapes),
        out_shape=[jax.ShapeDtypeStruct(s, jnp.bfloat16) for s in shapes],
        scratch_shapes=[pltpu.VMEM((width, width), jnp.bfloat16)],
        compiler_params=pltpu.CompilerParams(vmem_limit_bytes=16 * 2**20),
    )(table, *load(x))


def join_kernel(mine_ref, theirs_ref, *outs):
    for i, out in enumerate(outs):
        out[0] = mine_ref[i]
        out[1] = theirs_ref[i + 1]


def join(mine, theirs):
    count = mine.shape[0]
    shape = jax.ShapeDtypeStruct((2,) + mine.shape[1:], mine.dtype)
    return pl.pallas_call(
        join_kernel,
        in_specs=[VMEM] * 2,
        out_specs=[VMEM] * count,
        out_shape=[shape] * count,
        compiler_params=pltpu.CompilerParams(vmem_limit_bytes=16 * 2**20),
    )(mine, theirs)


def second_kernel(*refs):
    for i, ref in enumerate(refs[:-1]):
        refs[-1][i] = ref[1]


def second_blocks(*pieces):
    shape = jax.ShapeDtypeStruct((len(pieces),) + pieces[0].shape[1:], pieces[0].dtype)
    return pl.pallas_call(
        second_kernel,
        in_specs=[VMEM] * len(pieces),
        out_specs=VMEM,
        out_shape=shape,
        compiler_params=pltpu.CompilerParams(vmem_limit_bytes=16 * 2**20),
    )(*pieces)


def transform_kernel(*refs, skip, far, steps, width, added):
    table_ref, tables_ref, *refs = refs[skip:]
    if far:
        blocks = [(r.at[0], r.at[1]) for r in refs[: 2 * len(steps)]]
        refs = refs[2 * len(steps) :]
    else:
        own, theirs, *came, changed = refs[:10]
        blocks = [(own, theirs.at[0])]
        for d, r in zip(NEAR[1:], came):
            blocks.append((r.at[0], changed.at[EARLY.index(d)] if d in EARLY else r.at[1]))
        refs = refs[10:]
    before = refs[0] if added else None
    out_ref, held = refs[-2:]
    me = here()
    core, z = (me >> 2) & 1, me & 3
    x = (me >> 3) & 1 ^ (1 if far else 0)
    sign = jnp.where(me < Y, 1.0, -1.0).astype(jnp.float32)
    levs, channels = held.shape[2], held.shape[3] // 8
    whole = 2 * (WIDE + REST)

    def put(e, lev, row, lane, value):
        for i in range(value.shape[1] // 128):
            held[e, lane // 128 + i, lev, pl.ds(row, 8), :] = value[:, i * 128 : (i + 1) * 128]

    def stage(flip):
        for j, step in enumerate(steps):
            lev = (z ^ step) & (levs - 1)

            def both(half, at, size):
                a = blocks[j][half ^ flip][:, at : at + size].astype(jnp.float32)
                b = blocks[len(steps) + j][half ^ flip][:, at : at + size].astype(jnp.float32)
                return a + b, (a - b) * sign

            for half in range(2):
                for c in range(channels):
                    for e, value in enumerate(both(half, c * WIDE, WIDE)):
                        put(e, lev, c * 8, half * (WIDE + 2 * REST), value)
            for c in range(0, channels, 2):
                zero, one = [both(half, channels * WIDE + c * REST, 2 * REST) for half in range(2)]
                for e in range(2):
                    even = jnp.concatenate([zero[e][:, :REST], one[e][:, :REST]], 1)
                    odd = jnp.concatenate([zero[e][:, REST:], one[e][:, REST:]], 1)
                    put(e, lev, c * 8, WIDE, even)
                    put(e, lev, c * 8 + 8, WIDE, odd)

    for flip in range(2):
        pl.when(core == flip)(functools.partial(stage, flip))

    rows = levs * channels
    low = (z ^ steps[0]) < levs
    lanes = pl.ds(pl.multiple_of(x * whole, 128), whole)
    slot = lax.broadcasted_iota(jnp.int32, table_ref.shape, 1) - me * 4
    for s in range(4):
        pair = jnp.sum(jnp.where(slot == s, table_ref[...], 0), axis=1, keepdims=True)
        for e in range(2):
            tiles = [held.at[e, i].reshape(rows * 8, 128) for i in range(whole // 128)]
            picked = [
                jnp.concatenate([t[pl.ds(2 * s + w, rows, stride=8), :] for t in tiles], 1)
                for w in range(2)
            ]
            products = lax.dot_general(
                jnp.concatenate(picked, 0).astype(jnp.bfloat16),
                tables_ref[s, e, :, lanes],
                NT,
                preferred_element_type=jnp.float32,
            )
            count = (width - pair - e + 1) >> 1
            degree = lax.broadcasted_iota(jnp.int32, (rows, products.shape[1]), 1)
            chosen = jnp.where(degree < count, products[:rows], products[rows:])
            if levs < 4:
                parts = [jnp.where(low, chosen, 0.0), jnp.where(low, 0.0, chosen)]
                chosen = jnp.concatenate(parts, 0)
            if added:
                chosen = chosen + before[s, e]
            out_ref[s, e] = chosen.astype(out_ref.dtype)


def transform(table, tables, blocks, far, steps, width, before=None, last=False, rest=()):
    slots, _, degrees, lats = tables.shape
    channels = blocks[0].shape[-1] // (WIDE + REST)
    more = [] if before is None else [before]
    return pl.pallas_call(
        functools.partial(
            transform_kernel,
            skip=len(rest),
            far=far,
            steps=steps,
            width=width,
            added=before is not None,
        ),
        in_specs=[pl.BlockSpec(memory_space=pl.ANY)] * len(rest)
        + [VMEM] * (2 + len(blocks) + len(more)),
        out_specs=VMEM,
        out_shape=jax.ShapeDtypeStruct(
            (slots, 2, 4 * channels, degrees), jnp.bfloat16 if last else jnp.float32
        ),
        scratch_shapes=[
            pltpu.VMEM((2, 2 * (WIDE + REST) // 128, len(steps), channels * 8, 128), jnp.float32)
        ],
        compiler_params=pltpu.CompilerParams(vmem_limit_bytes=20 * 2**20),
    )(*rest, table, tables, *blocks, *more)


def send(piece, distance):
    count = lax.axis_size("lat") * lax.axis_size("lev")
    return lax.ppermute(piece, ("lat", "lev"), [(i, i ^ distance) for i in range(count)])


def on_block(fourier, table, legendre):
    width = fourier.shape[2]
    entries = table.reshape(1, -1)
    mine, theirs, own, *early = pick(entries, fourier.transpose(1, 0, 2))
    got = {d: send(piece, d) for d, piece in zip(EARLY, early)}
    theirs = send(theirs, CORE)
    ready = dict(zip(JOINED, join(mine, theirs)))
    got.update({d: send(ready[d], d) for d in ORDER})
    came = [got[d] for d in EARLY]
    *came, got[ORDER[0]] = lax.optimization_barrier((*came, got[ORDER[0]]))
    changed = send(second_blocks(*came), CORE)
    near = [own, theirs] + [got[d] for d in NEAR[1:]] + [changed]
    total = transform(entries, legendre, near, False, (0, 1, 2, 3), width)
    far = [got[d] for d in FAR]
    rest = list(got.values())
    rest.insert(len(rest) - LATE, changed)
    return transform(
        entries, legendre, far, True, (0, 1, 2, 3), width, total, True, rest
    )


def row_counts(table, slot_count, wavenumbers):
    position = lax.axis_index(("lat", "lev")) * slot_count
    owned = lax.dynamic_slice_in_dim(table, position, slot_count)
    parity = jnp.arange(2, dtype=jnp.int32)
    return (wavenumbers - owned[:, None] - parity[None, :] + 1) // 2


def on_any(fourier, table, legendre):
    lat_count, lev_count = lax.axis_size("lat"), lax.axis_size("lev")
    devices, half_lat = lat_count * lev_count, lat_count // 2
    lat_rows, channels, wavenumbers = fourier.shape
    slot_count, _, degree_rows, _ = legendre.shape
    columns = jnp.stack([table, wavenumbers - 1 - table], axis=1).reshape(-1)
    picked = jnp.take(fourier, columns, axis=2)
    shaped = picked.reshape((1, lat_rows, channels, devices, wavenumbers // devices))
    arrived = lax.all_to_all(shaped, ("lat", "lev"), split_axis=3, concat_axis=0, tiled=True)
    halves = arrived.reshape(2, half_lat, lev_count, lat_rows, channels, slot_count, 2)
    north, south = halves[0].astype(jnp.float32), halves[1].astype(jnp.float32)
    merged = jnp.stack([north + south, north - south]).astype(jnp.bfloat16)
    tables = legendre.reshape(slot_count, 2, degree_rows, half_lat, lat_rows)
    products = jnp.einsum(
        "ealbcsw,serab->selcwr", merged, tables, preferred_element_type=jnp.float32
    )
    products = products.reshape(slot_count, 2, lev_count * channels, 2, degree_rows)
    first = row_counts(table, slot_count, wavenumbers)
    in_first = jnp.arange(degree_rows, dtype=jnp.int32)[None, None, :] < first[:, :, None]
    spectral = jnp.where(in_first[:, :, None, :], products[:, :, :, 0], products[:, :, :, 1])
    return spectral.astype(jnp.bfloat16)


def solution(mesh):
    in_specs = (P("lat", "lev", None), P(), P(("lat", "lev"), None, None, None))
    out_specs = P(("lat", "lev"), None, None, None)
    on_device = on_block if dict(mesh.shape) == {"lat": 8, "lev": 4} else on_any
    return jax.shard_map(
        on_device, mesh=mesh, in_specs=in_specs, out_specs=out_specs, check_vma=False
    )
```

```python
import functools

import jax
import jax.numpy as jnp
from jax import lax
from jax.experimental import pallas as pl
from jax.experimental.pallas import tpu as pltpu
from jax.sharding import PartitionSpec as P

NT = (((1,), (1,)), ((), ()))
VMEM = pl.BlockSpec(memory_space=pltpu.VMEM)
HBM = pl.BlockSpec(memory_space=pltpu.HBM)
Y, X, CORE = 16, 8, 4
NEAR = (0, 1, 2, 3, Y, Y + 1, Y + 2, Y + 3)
FAR = tuple(X + d for d in NEAR)
EARLY = (3, 2)
JOINED = tuple(d for d in NEAR[1:] + FAR if d not in EARLY)
LATE = 4
ORDER = (17, 16, 18, 1, 19, 8, 9, 26, 24, 27, 10, 25, 11)
WIDE, REST = 256, 64


def here():
    return lax.axis_index("lat") * lax.axis_size("lev") + lax.axis_index("lev")


def load_kernel(x_ref, wide_ref, rest_ref, sems):
    core = (here() >> 2) & 1
    first = pl.multiple_of(core * REST, REST)
    last = pl.multiple_of((1 - core) * WIDE, REST)
    copies = [
        pltpu.make_async_copy(x_ref.at[:, pl.ds(first, WIDE)], wide_ref, sems.at[0]),
        pltpu.make_async_copy(x_ref.at[:, pl.ds(last, REST)], rest_ref, sems.at[1]),
    ]
    for copy in copies:
        copy.start()
    for copy in copies:
        copy.wait()


def load(x):
    channels, _, width = x.shape
    shapes = [(channels, WIDE, width), (channels, REST, width)]
    return pl.pallas_call(
        load_kernel,
        in_specs=[HBM],
        out_specs=[VMEM] * 2,
        out_shape=[jax.ShapeDtypeStruct(s, x.dtype) for s in shapes],
        scratch_shapes=[pltpu.SemaphoreType.DMA((2,))],
        cost_estimate=pl.CostEstimate(flops=10**9, bytes_accessed=4 * x.size, transcendentals=0),
        compiler_params=pltpu.CompilerParams(vmem_limit_bytes=51 * 2**20),
    )(x)


def pick_kernel(table_ref, wide_ref, rest_ref, mine_ref, theirs_ref, *refs, early):
    early_refs, (onehot,) = refs[:early], refs[early:]
    width = onehot.shape[0]
    channels = wide_ref.shape[0]
    me = here()
    row = lax.broadcasted_iota(jnp.int32, (width, 1), 0)
    block = row >> 3
    distance = ((block >> 2) & 1) * Y | ((block >> 3) & 1) * X | (block >> 4) * CORE | block & 3
    slot = (distance ^ me) * 4 + ((row >> 1) & 3)
    lane = lax.broadcasted_iota(jnp.int32, (width, table_ref.shape[1]), 1)
    pair = jnp.sum(jnp.where(lane == slot, table_ref[...], 0), axis=1, keepdims=True)
    column = jnp.where(row & 1 == 1, width - 1 - pair, pair)
    at = lax.broadcasted_iota(jnp.int32, (width, width), 1)
    onehot[...] = jnp.where(at == column, 1.0, 0.0).astype(jnp.bfloat16)

    def emit(x, lanes):
        picked = lax.dot_general(onehot[...], x, NT, preferred_element_type=jnp.float32)
        picked = picked.astype(jnp.bfloat16).reshape(32, 8, picked.shape[1])
        for i, d in enumerate(JOINED):
            mine_ref[i, :, lanes] = picked[(NEAR + FAR).index(d)]
            theirs_ref[i + 1, :, lanes] = picked[16 + (NEAR + FAR).index(d)]
        theirs_ref[0, :, lanes] = picked[16]
        early_refs[0][:, lanes] = picked[0]
        for i, d in enumerate(EARLY):
            early_refs[i + 1][0, :, lanes] = picked[NEAR.index(d)]
            early_refs[i + 1][1, :, lanes] = picked[16 + NEAR.index(d)]

    for c in range(0, channels, 2):
        x = wide_ref[c : c + 2].reshape(2 * WIDE, width)
        emit(x, pl.ds(c * WIDE, 2 * WIDE))
    emit(rest_ref[...].reshape(channels * REST, width), pl.ds(channels * WIDE, channels * REST))


def pick(table, x):
    channels, lat_rows, width = x.shape
    block = (8, channels * lat_rows)
    early = 1 + len(EARLY)
    shapes = [(len(JOINED),) + block, (len(JOINED) + 1,) + block, block] + [(2,) + block] * len(EARLY)
    return pl.pallas_call(
        functools.partial(pick_kernel, early=early),
        in_specs=[VMEM] * 3,
        out_specs=[VMEM] * len(shapes),
        out_shape=[jax.ShapeDtypeStruct(s, jnp.bfloat16) for s in shapes],
        scratch_shapes=[pltpu.VMEM((width, width), jnp.bfloat16)],
        compiler_params=pltpu.CompilerParams(vmem_limit_bytes=16 * 2**20),
    )(table, *load(x))


def join_kernel(mine_ref, theirs_ref, *outs):
    for i, out in enumerate(outs):
        out[0] = mine_ref[i]
        out[1] = theirs_ref[i + 1]


def join(mine, theirs):
    count = mine.shape[0]
    shape = jax.ShapeDtypeStruct((2,) + mine.shape[1:], mine.dtype)
    return pl.pallas_call(
        join_kernel,
        in_specs=[VMEM] * 2,
        out_specs=[VMEM] * count,
        out_shape=[shape] * count,
        compiler_params=pltpu.CompilerParams(vmem_limit_bytes=16 * 2**20),
    )(mine, theirs)


def second_kernel(*refs):
    for i, ref in enumerate(refs[:-1]):
        refs[-1][i] = ref[1]


def second_blocks(*pieces):
    shape = jax.ShapeDtypeStruct((len(pieces),) + pieces[0].shape[1:], pieces[0].dtype)
    return pl.pallas_call(
        second_kernel,
        in_specs=[VMEM] * len(pieces),
        out_specs=VMEM,
        out_shape=shape,
        compiler_params=pltpu.CompilerParams(vmem_limit_bytes=16 * 2**20),
    )(*pieces)


def transform_kernel(*refs, skip, far, steps, width, added):
    table_ref, tables_ref, *refs = refs[skip:]
    if far:
        blocks = [(r.at[0], r.at[1]) for r in refs[: 2 * len(steps)]]
        refs = refs[2 * len(steps) :]
    else:
        own, theirs, *came, changed = refs[:10]
        blocks = [(own, theirs.at[0])]
        for d, r in zip(NEAR[1:], came):
            blocks.append((r.at[0], changed.at[EARLY.index(d)] if d in EARLY else r.at[1]))
        refs = refs[10:]
    before = refs[0] if added else None
    out_ref, held = refs[-2:]
    me = here()
    core, z = (me >> 2) & 1, me & 3
    x = (me >> 3) & 1 ^ (1 if far else 0)
    sign = jnp.where(me < Y, 1.0, -1.0).astype(jnp.float32)
    levs, channels = held.shape[2], held.shape[3] // 8
    whole = 2 * (WIDE + REST)

    def put(e, lev, row, lane, value):
        for i in range(value.shape[1] // 128):
            held[e, lane // 128 + i, lev, pl.ds(row, 8), :] = value[:, i * 128 : (i + 1) * 128]

    def stage(flip):
        for j, step in enumerate(steps):
            lev = (z ^ step) & (levs - 1)

            def both(half, at, size):
                a = blocks[j][half ^ flip][:, at : at + size].astype(jnp.float32)
                b = blocks[len(steps) + j][half ^ flip][:, at : at + size].astype(jnp.float32)
                return a + b, (a - b) * sign

            for half in range(2):
                for c in range(channels):
                    for e, value in enumerate(both(half, c * WIDE, WIDE)):
                        put(e, lev, c * 8, half * (WIDE + 2 * REST), value)
            for c in range(0, channels, 2):
                zero, one = [both(half, channels * WIDE + c * REST, 2 * REST) for half in range(2)]
                for e in range(2):
                    even = jnp.concatenate([zero[e][:, :REST], one[e][:, :REST]], 1)
                    odd = jnp.concatenate([zero[e][:, REST:], one[e][:, REST:]], 1)
                    put(e, lev, c * 8, WIDE, even)
                    put(e, lev, c * 8 + 8, WIDE, odd)

    for flip in range(2):
        pl.when(core == flip)(functools.partial(stage, flip))

    rows = levs * channels
    low = (z ^ steps[0]) < levs
    lanes = pl.ds(pl.multiple_of(x * whole, 128), whole)
    slot = lax.broadcasted_iota(jnp.int32, table_ref.shape, 1) - me * 4
    for s in range(4):
        pair = jnp.sum(jnp.where(slot == s, table_ref[...], 0), axis=1, keepdims=True)
        for e in range(2):
            tiles = [held.at[e, i].reshape(rows * 8, 128) for i in range(whole // 128)]
            picked = [
                jnp.concatenate([t[pl.ds(2 * s + w, rows, stride=8), :] for t in tiles], 1)
                for w in range(2)
            ]
            products = lax.dot_general(
                jnp.concatenate(picked, 0).astype(jnp.bfloat16),
                tables_ref[s, e, :, lanes],
                NT,
                preferred_element_type=jnp.float32,
            )
            count = (width - pair - e + 1) >> 1
            degree = lax.broadcasted_iota(jnp.int32, (rows, products.shape[1]), 1)
            chosen = jnp.where(degree < count, products[:rows], products[rows:])
            if levs < 4:
                parts = [jnp.where(low, chosen, 0.0), jnp.where(low, 0.0, chosen)]
                chosen = jnp.concatenate(parts, 0)
            if added:
                chosen = chosen + before[s, e]
            out_ref[s, e] = chosen.astype(out_ref.dtype)


def transform(table, tables, blocks, far, steps, width, before=None, last=False, rest=()):
    slots, _, degrees, lats = tables.shape
    channels = blocks[0].shape[-1] // (WIDE + REST)
    more = [] if before is None else [before]
    return pl.pallas_call(
        functools.partial(
            transform_kernel,
            skip=len(rest),
            far=far,
            steps=steps,
            width=width,
            added=before is not None,
        ),
        in_specs=[pl.BlockSpec(memory_space=pl.ANY)] * len(rest)
        + [VMEM] * (2 + len(blocks) + len(more)),
        out_specs=VMEM,
        out_shape=jax.ShapeDtypeStruct(
            (slots, 2, 4 * channels, degrees), jnp.bfloat16 if last else jnp.float32
        ),
        scratch_shapes=[
            pltpu.VMEM((2, 2 * (WIDE + REST) // 128, len(steps), channels * 8, 128), jnp.float32)
        ],
        compiler_params=pltpu.CompilerParams(vmem_limit_bytes=20 * 2**20),
    )(*rest, table, tables, *blocks, *more)


def send(piece, distance):
    count = lax.axis_size("lat") * lax.axis_size("lev")
    return lax.ppermute(piece, ("lat", "lev"), [(i, i ^ distance) for i in range(count)])


def on_block(fourier, table, legendre):
    width = fourier.shape[2]
    entries = table.reshape(1, -1)
    mine, theirs, own, *early = pick(entries, fourier.transpose(1, 0, 2))
    got = {d: send(piece, d) for d, piece in zip(EARLY, early)}
    theirs = send(theirs, CORE)
    ready = dict(zip(JOINED, join(mine, theirs)))
    got.update({d: send(ready[d], d) for d in ORDER})
    came = [got[d] for d in EARLY]
    *came, got[ORDER[0]] = lax.optimization_barrier((*came, got[ORDER[0]]))
    changed = send(second_blocks(*came), CORE)
    near = [own, theirs] + [got[d] for d in NEAR[1:]] + [changed]
    total = transform(entries, legendre, near, False, (0, 1, 2, 3), width)
    far = [got[d] for d in FAR]
    rest = list(got.values())
    rest.insert(len(rest) - LATE, changed)
    return transform(
        entries, legendre, far, True, (0, 1, 2, 3), width, total, True, rest
    )


def row_counts(table, slot_count, wavenumbers):
    position = lax.axis_index(("lat", "lev")) * slot_count
    owned = lax.dynamic_slice_in_dim(table, position, slot_count)
    parity = jnp.arange(2, dtype=jnp.int32)
    return (wavenumbers - owned[:, None] - parity[None, :] + 1) // 2


def on_any(fourier, table, legendre):
    lat_count, lev_count = lax.axis_size("lat"), lax.axis_size("lev")
    devices, half_lat = lat_count * lev_count, lat_count // 2
    lat_rows, channels, wavenumbers = fourier.shape
    slot_count, _, degree_rows, _ = legendre.shape
    columns = jnp.stack([table, wavenumbers - 1 - table], axis=1).reshape(-1)
    picked = jnp.take(fourier, columns, axis=2)
    shaped = picked.reshape((1, lat_rows, channels, devices, wavenumbers // devices))
    arrived = lax.all_to_all(shaped, ("lat", "lev"), split_axis=3, concat_axis=0, tiled=True)
    halves = arrived.reshape(2, half_lat, lev_count, lat_rows, channels, slot_count, 2)
    north, south = halves[0].astype(jnp.float32), halves[1].astype(jnp.float32)
    merged = jnp.stack([north + south, north - south]).astype(jnp.bfloat16)
    tables = legendre.reshape(slot_count, 2, degree_rows, half_lat, lat_rows)
    products = jnp.einsum(
        "ealbcsw,serab->selcwr", merged, tables, preferred_element_type=jnp.float32
    )
    products = products.reshape(slot_count, 2, lev_count * channels, 2, degree_rows)
    first = row_counts(table, slot_count, wavenumbers)
    in_first = jnp.arange(degree_rows, dtype=jnp.int32)[None, None, :] < first[:, :, None]
    spectral = jnp.where(in_first[:, :, None, :], products[:, :, :, 0], products[:, :, :, 1])
    return spectral.astype(jnp.bfloat16)


def solution(mesh):
    in_specs = (P("lat", "lev", None), P(), P(("lat", "lev"), None, None, None))
    out_specs = P(("lat", "lev"), None, None, None)
    on_device = on_block if dict(mesh.shape) == {"lat": 8, "lev": 4} else on_any
    return jax.shard_map(
        on_device, mesh=mesh, in_specs=in_specs, out_specs=out_specs, check_vma=False
    )
```

```python
import functools

import jax
import jax.numpy as jnp
from jax import lax
from jax.experimental import pallas as pl
from jax.experimental.pallas import tpu as pltpu
from jax.sharding import PartitionSpec as P

NT = (((1,), (1,)), ((), ()))
VMEM = pl.BlockSpec(memory_space=pltpu.VMEM)
HBM = pl.BlockSpec(memory_space=pltpu.HBM)
Y, X, CORE = 16, 8, 4
NEAR = (0, 1, 2, 3, Y, Y + 1, Y + 2, Y + 3)
FAR = tuple(X + d for d in NEAR)
EARLY = (3, 2)
JOINED = tuple(d for d in NEAR[1:] + FAR if d not in EARLY)
LATE = 4
ORDER = (17, 16, 18, 1, 19, 8, 9, 26, 24, 27, 10, 25, 11)
WIDE, REST = 256, 64


def here():
    return lax.axis_index("lat") * lax.axis_size("lev") + lax.axis_index("lev")


def load_kernel(x_ref, wide_ref, rest_ref, sems):
    core = (here() >> 2) & 1
    first = pl.multiple_of(core * REST, REST)
    last = pl.multiple_of((1 - core) * WIDE, REST)
    copies = [
        pltpu.make_async_copy(x_ref.at[:, pl.ds(first, WIDE)], wide_ref, sems.at[0]),
        pltpu.make_async_copy(x_ref.at[:, pl.ds(last, REST)], rest_ref, sems.at[1]),
    ]
    for copy in copies:
        copy.start()
    for copy in copies:
        copy.wait()


def load(x):
    channels, _, width = x.shape
    shapes = [(channels, WIDE, width), (channels, REST, width)]
    return pl.pallas_call(
        load_kernel,
        in_specs=[HBM],
        out_specs=[VMEM] * 2,
        out_shape=[jax.ShapeDtypeStruct(s, x.dtype) for s in shapes],
        scratch_shapes=[pltpu.SemaphoreType.DMA((2,))],
        cost_estimate=pl.CostEstimate(flops=10**9, bytes_accessed=4 * x.size, transcendentals=0),
        compiler_params=pltpu.CompilerParams(vmem_limit_bytes=51 * 2**20),
    )(x)


def pick_kernel(table_ref, wide_ref, rest_ref, mine_ref, theirs_ref, *refs, early):
    early_refs, (onehot,) = refs[:early], refs[early:]
    width = onehot.shape[0]
    channels = wide_ref.shape[0]
    me = here()
    row = lax.broadcasted_iota(jnp.int32, (width, 1), 0)
    block = row >> 3
    distance = ((block >> 2) & 1) * Y | ((block >> 3) & 1) * X | (block >> 4) * CORE | block & 3
    slot = (distance ^ me) * 4 + ((row >> 1) & 3)
    lane = lax.broadcasted_iota(jnp.int32, (width, table_ref.shape[1]), 1)
    pair = jnp.sum(jnp.where(lane == slot, table_ref[...], 0), axis=1, keepdims=True)
    column = jnp.where(row & 1 == 1, width - 1 - pair, pair)
    at = lax.broadcasted_iota(jnp.int32, (width, width), 1)
    onehot[...] = jnp.where(at == column, 1.0, 0.0).astype(jnp.bfloat16)

    def emit(x, lanes):
        picked = lax.dot_general(onehot[...], x, NT, preferred_element_type=jnp.float32)
        picked = picked.astype(jnp.bfloat16).reshape(32, 8, picked.shape[1])
        for i, d in enumerate(JOINED):
            mine_ref[i, :, lanes] = picked[(NEAR + FAR).index(d)]
            theirs_ref[i + 1, :, lanes] = picked[16 + (NEAR + FAR).index(d)]
        theirs_ref[0, :, lanes] = picked[16]
        early_refs[0][:, lanes] = picked[0]
        for i, d in enumerate(EARLY):
            early_refs[i + 1][0, :, lanes] = picked[NEAR.index(d)]
            early_refs[i + 1][1, :, lanes] = picked[16 + NEAR.index(d)]

    for c in range(0, channels, 2):
        x = wide_ref[c : c + 2].reshape(2 * WIDE, width)
        emit(x, pl.ds(c * WIDE, 2 * WIDE))
    emit(rest_ref[...].reshape(channels * REST, width), pl.ds(channels * WIDE, channels * REST))


def pick(table, x):
    channels, lat_rows, width = x.shape
    block = (8, channels * lat_rows)
    early = 1 + len(EARLY)
    shapes = [(len(JOINED),) + block, (len(JOINED) + 1,) + block, block] + [(2,) + block] * len(EARLY)
    return pl.pallas_call(
        functools.partial(pick_kernel, early=early),
        in_specs=[VMEM] * 3,
        out_specs=[VMEM] * len(shapes),
        out_shape=[jax.ShapeDtypeStruct(s, jnp.bfloat16) for s in shapes],
        scratch_shapes=[pltpu.VMEM((width, width), jnp.bfloat16)],
        compiler_params=pltpu.CompilerParams(vmem_limit_bytes=16 * 2**20),
    )(table, *load(x))


def join_kernel(mine_ref, theirs_ref, *outs):
    for i, out in enumerate(outs):
        out[0] = mine_ref[i]
        out[1] = theirs_ref[i + 1]


def join(mine, theirs):
    count = mine.shape[0]
    shape = jax.ShapeDtypeStruct((2,) + mine.shape[1:], mine.dtype)
    return pl.pallas_call(
        join_kernel,
        in_specs=[VMEM] * 2,
        out_specs=[VMEM] * count,
        out_shape=[shape] * count,
        compiler_params=pltpu.CompilerParams(vmem_limit_bytes=16 * 2**20),
    )(mine, theirs)


def second_kernel(*refs):
    for i, ref in enumerate(refs[:-1]):
        refs[-1][i] = ref[1]


def second_blocks(*pieces):
    shape = jax.ShapeDtypeStruct((len(pieces),) + pieces[0].shape[1:], pieces[0].dtype)
    return pl.pallas_call(
        second_kernel,
        in_specs=[VMEM] * len(pieces),
        out_specs=VMEM,
        out_shape=shape,
        compiler_params=pltpu.CompilerParams(vmem_limit_bytes=16 * 2**20),
    )(*pieces)


def transform_kernel(*refs, skip, far, steps, width, added):
    table_ref, tables_ref, *refs = refs[skip:]
    if far:
        blocks = [(r.at[0], r.at[1]) for r in refs[: 2 * len(steps)]]
        refs = refs[2 * len(steps) :]
    else:
        own, theirs, *came, changed = refs[:10]
        blocks = [(own, theirs.at[0])]
        for d, r in zip(NEAR[1:], came):
            blocks.append((r.at[0], changed.at[EARLY.index(d)] if d in EARLY else r.at[1]))
        refs = refs[10:]
    before = refs[0] if added else None
    out_ref, held = refs[-2:]
    me = here()
    core, z = (me >> 2) & 1, me & 3
    x = (me >> 3) & 1 ^ (1 if far else 0)
    sign = jnp.where(me < Y, 1.0, -1.0).astype(jnp.float32)
    levs, channels = held.shape[2], held.shape[3] // 8
    whole = 2 * (WIDE + REST)

    def put(e, lev, row, lane, value):
        for i in range(value.shape[1] // 128):
            held[e, lane // 128 + i, lev, pl.ds(row, 8), :] = value[:, i * 128 : (i + 1) * 128]

    def stage(flip):
        for j, step in enumerate(steps):
            lev = (z ^ step) & (levs - 1)

            def both(half, at, size):
                a = blocks[j][half ^ flip][:, at : at + size].astype(jnp.float32)
                b = blocks[len(steps) + j][half ^ flip][:, at : at + size].astype(jnp.float32)
                return a + b, (a - b) * sign

            for half in range(2):
                for c in range(channels):
                    for e, value in enumerate(both(half, c * WIDE, WIDE)):
                        put(e, lev, c * 8, half * (WIDE + 2 * REST), value)
            for c in range(0, channels, 2):
                zero, one = [both(half, channels * WIDE + c * REST, 2 * REST) for half in range(2)]
                for e in range(2):
                    even = jnp.concatenate([zero[e][:, :REST], one[e][:, :REST]], 1)
                    odd = jnp.concatenate([zero[e][:, REST:], one[e][:, REST:]], 1)
                    put(e, lev, c * 8, WIDE, even)
                    put(e, lev, c * 8 + 8, WIDE, odd)

    for flip in range(2):
        pl.when(core == flip)(functools.partial(stage, flip))

    rows = levs * channels
    low = (z ^ steps[0]) < levs
    lanes = pl.ds(pl.multiple_of(x * whole, 128), whole)
    slot = lax.broadcasted_iota(jnp.int32, table_ref.shape, 1) - me * 4
    for s in range(4):
        pair = jnp.sum(jnp.where(slot == s, table_ref[...], 0), axis=1, keepdims=True)
        for e in range(2):
            tiles = [held.at[e, i].reshape(rows * 8, 128) for i in range(whole // 128)]
            picked = [
                jnp.concatenate([t[pl.ds(2 * s + w, rows, stride=8), :] for t in tiles], 1)
                for w in range(2)
            ]
            even = tables_ref.shape[2] - 1
            products = lax.dot_general(
                jnp.concatenate(picked, 0).astype(jnp.bfloat16),
                tables_ref[s, e, :even, lanes],
                NT,
                preferred_element_type=jnp.float32,
            )
            row = tables_ref[s, e, even:, lanes].astype(jnp.float32)
            second = picked[1].astype(jnp.bfloat16).astype(jnp.float32)
            final = jnp.sum(second * row, axis=1, keepdims=True)
            count = (width - pair - e + 1) >> 1
            degree = lax.broadcasted_iota(jnp.int32, (rows, even), 1)
            chosen = jnp.where(degree < count, products[:rows], products[rows:])
            chosen = jnp.concatenate([chosen, final], 1)
            if levs < 4:
                parts = [jnp.where(low, chosen, 0.0), jnp.where(low, 0.0, chosen)]
                chosen = jnp.concatenate(parts, 0)
            if added:
                chosen = chosen + before[s, e]
            out_ref[s, e] = chosen.astype(out_ref.dtype)


def transform(table, tables, blocks, far, steps, width, before=None, last=False, rest=()):
    slots, _, degrees, lats = tables.shape
    channels = blocks[0].shape[-1] // (WIDE + REST)
    more = [] if before is None else [before]
    return pl.pallas_call(
        functools.partial(
            transform_kernel,
            skip=len(rest),
            far=far,
            steps=steps,
            width=width,
            added=before is not None,
        ),
        in_specs=[pl.BlockSpec(memory_space=pl.ANY)] * len(rest)
        + [VMEM] * (2 + len(blocks) + len(more)),
        out_specs=VMEM,
        out_shape=jax.ShapeDtypeStruct(
            (slots, 2, 4 * channels, degrees), jnp.bfloat16 if last else jnp.float32
        ),
        scratch_shapes=[
            pltpu.VMEM((2, 2 * (WIDE + REST) // 128, len(steps), channels * 8, 128), jnp.float32)
        ],
        compiler_params=pltpu.CompilerParams(vmem_limit_bytes=20 * 2**20),
    )(*rest, table, tables, *blocks, *more)


def send(piece, distance):
    count = lax.axis_size("lat") * lax.axis_size("lev")
    return lax.ppermute(piece, ("lat", "lev"), [(i, i ^ distance) for i in range(count)])


def on_block(fourier, table, legendre):
    width = fourier.shape[2]
    entries = table.reshape(1, -1)
    mine, theirs, own, *early = pick(entries, fourier.transpose(1, 0, 2))
    got = {d: send(piece, d) for d, piece in zip(EARLY, early)}
    theirs = send(theirs, CORE)
    ready = dict(zip(JOINED, join(mine, theirs)))
    got.update({d: send(ready[d], d) for d in ORDER})
    came = [got[d] for d in EARLY]
    *came, got[ORDER[0]] = lax.optimization_barrier((*came, got[ORDER[0]]))
    changed = send(second_blocks(*came), CORE)
    near = [own, theirs] + [got[d] for d in NEAR[1:]] + [changed]
    total = transform(entries, legendre, near, False, (0, 1, 2, 3), width)
    far = [got[d] for d in FAR]
    rest = list(got.values())
    rest.insert(len(rest) - LATE, changed)
    return transform(
        entries, legendre, far, True, (0, 1, 2, 3), width, total, True, rest
    )


def row_counts(table, slot_count, wavenumbers):
    position = lax.axis_index(("lat", "lev")) * slot_count
    owned = lax.dynamic_slice_in_dim(table, position, slot_count)
    parity = jnp.arange(2, dtype=jnp.int32)
    return (wavenumbers - owned[:, None] - parity[None, :] + 1) // 2


def on_any(fourier, table, legendre):
    lat_count, lev_count = lax.axis_size("lat"), lax.axis_size("lev")
    devices, half_lat = lat_count * lev_count, lat_count // 2
    lat_rows, channels, wavenumbers = fourier.shape
    slot_count, _, degree_rows, _ = legendre.shape
    columns = jnp.stack([table, wavenumbers - 1 - table], axis=1).reshape(-1)
    picked = jnp.take(fourier, columns, axis=2)
    shaped = picked.reshape((1, lat_rows, channels, devices, wavenumbers // devices))
    arrived = lax.all_to_all(shaped, ("lat", "lev"), split_axis=3, concat_axis=0, tiled=True)
    halves = arrived.reshape(2, half_lat, lev_count, lat_rows, channels, slot_count, 2)
    north, south = halves[0].astype(jnp.float32), halves[1].astype(jnp.float32)
    merged = jnp.stack([north + south, north - south]).astype(jnp.bfloat16)
    tables = legendre.reshape(slot_count, 2, degree_rows, half_lat, lat_rows)
    products = jnp.einsum(
        "ealbcsw,serab->selcwr", merged, tables, preferred_element_type=jnp.float32
    )
    products = products.reshape(slot_count, 2, lev_count * channels, 2, degree_rows)
    first = row_counts(table, slot_count, wavenumbers)
    in_first = jnp.arange(degree_rows, dtype=jnp.int32)[None, None, :] < first[:, :, None]
    spectral = jnp.where(in_first[:, :, None, :], products[:, :, :, 0], products[:, :, :, 1])
    return spectral.astype(jnp.bfloat16)


def solution(mesh):
    in_specs = (P("lat", "lev", None), P(), P(("lat", "lev"), None, None, None))
    out_specs = P(("lat", "lev"), None, None, None)
    on_device = on_block if dict(mesh.shape) == {"lat": 8, "lev": 4} else on_any
    return jax.shard_map(
        on_device, mesh=mesh, in_specs=in_specs, out_specs=out_specs, check_vma=False
    )
```

```python
import functools

import jax
import jax.numpy as jnp
from jax import lax
from jax.experimental import pallas as pl
from jax.experimental.pallas import tpu as pltpu
from jax.sharding import PartitionSpec as P

NT = (((1,), (1,)), ((), ()))
VMEM = pl.BlockSpec(memory_space=pltpu.VMEM)
HBM = pl.BlockSpec(memory_space=pltpu.HBM)
Y, X, CORE = 16, 8, 4
NEAR = (0, 1, 2, 3, Y, Y + 1, Y + 2, Y + 3)
FAR = tuple(X + d for d in NEAR)
EARLY = (3, 2)
JOINED = tuple(d for d in NEAR[1:] + FAR if d not in EARLY)
LATE = 4
ORDER = (17, 16, 18, 1, 19, 8, 9, 26, 24, 27, 10, 11, 25)
WIDE, REST = 256, 64


def here():
    return lax.axis_index("lat") * lax.axis_size("lev") + lax.axis_index("lev")


def load_kernel(x_ref, wide_ref, rest_ref, sems):
    core = (here() >> 2) & 1
    first = pl.multiple_of(core * REST, REST)
    last = pl.multiple_of((1 - core) * WIDE, REST)
    copies = [
        pltpu.make_async_copy(x_ref.at[:, pl.ds(first, WIDE)], wide_ref, sems.at[0]),
        pltpu.make_async_copy(x_ref.at[:, pl.ds(last, REST)], rest_ref, sems.at[1]),
    ]
    for copy in copies:
        copy.start()
    for copy in copies:
        copy.wait()


def load(x):
    channels, _, width = x.shape
    shapes = [(channels, WIDE, width), (channels, REST, width)]
    return pl.pallas_call(
        load_kernel,
        in_specs=[HBM],
        out_specs=[VMEM] * 2,
        out_shape=[jax.ShapeDtypeStruct(s, x.dtype) for s in shapes],
        scratch_shapes=[pltpu.SemaphoreType.DMA((2,))],
        cost_estimate=pl.CostEstimate(flops=10**9, bytes_accessed=4 * x.size, transcendentals=0),
        compiler_params=pltpu.CompilerParams(vmem_limit_bytes=51 * 2**20),
    )(x)


def pick_kernel(table_ref, wide_ref, rest_ref, mine_ref, theirs_ref, *refs, early):
    early_refs, (onehot,) = refs[:early], refs[early:]
    width = onehot.shape[0]
    channels = wide_ref.shape[0]
    me = here()
    row = lax.broadcasted_iota(jnp.int32, (width, 1), 0)
    block = row >> 3
    distance = ((block >> 2) & 1) * Y | ((block >> 3) & 1) * X | (block >> 4) * CORE | block & 3
    slot = (distance ^ me) * 4 + ((row >> 1) & 3)
    lane = lax.broadcasted_iota(jnp.int32, (width, table_ref.shape[1]), 1)
    pair = jnp.sum(jnp.where(lane == slot, table_ref[...], 0), axis=1, keepdims=True)
    column = jnp.where(row & 1 == 1, width - 1 - pair, pair)
    at = lax.broadcasted_iota(jnp.int32, (width, width), 1)
    onehot[...] = jnp.where(at == column, 1.0, 0.0).astype(jnp.bfloat16)

    def emit(x, lanes):
        picked = lax.dot_general(onehot[...], x, NT, preferred_element_type=jnp.float32)
        picked = picked.astype(jnp.bfloat16).reshape(32, 8, picked.shape[1])
        for i, d in enumerate(JOINED):
            mine_ref[i, :, lanes] = picked[(NEAR + FAR).index(d)]
            theirs_ref[i + 1, :, lanes] = picked[16 + (NEAR + FAR).index(d)]
        theirs_ref[0, :, lanes] = picked[16]
        early_refs[0][:, lanes] = picked[0]
        for i, d in enumerate(EARLY):
            early_refs[i + 1][0, :, lanes] = picked[NEAR.index(d)]
            early_refs[i + 1][1, :, lanes] = picked[16 + NEAR.index(d)]

    for c in range(0, channels, 2):
        x = wide_ref[c : c + 2].reshape(2 * WIDE, width)
        emit(x, pl.ds(c * WIDE, 2 * WIDE))
    emit(rest_ref[...].reshape(channels * REST, width), pl.ds(channels * WIDE, channels * REST))


def pick(table, x):
    channels, lat_rows, width = x.shape
    block = (8, channels * lat_rows)
    early = 1 + len(EARLY)
    shapes = [(len(JOINED),) + block, (len(JOINED) + 1,) + block, block] + [(2,) + block] * len(EARLY)
    return pl.pallas_call(
        functools.partial(pick_kernel, early=early),
        in_specs=[VMEM] * 3,
        out_specs=[VMEM] * len(shapes),
        out_shape=[jax.ShapeDtypeStruct(s, jnp.bfloat16) for s in shapes],
        scratch_shapes=[pltpu.VMEM((width, width), jnp.bfloat16)],
        compiler_params=pltpu.CompilerParams(vmem_limit_bytes=16 * 2**20),
    )(table, *load(x))


def join_kernel(mine_ref, theirs_ref, *outs):
    for i, out in enumerate(outs):
        out[0] = mine_ref[i]
        out[1] = theirs_ref[i + 1]


def join(mine, theirs):
    count = mine.shape[0]
    shape = jax.ShapeDtypeStruct((2,) + mine.shape[1:], mine.dtype)
    return pl.pallas_call(
        join_kernel,
        in_specs=[VMEM] * 2,
        out_specs=[VMEM] * count,
        out_shape=[shape] * count,
        compiler_params=pltpu.CompilerParams(vmem_limit_bytes=16 * 2**20),
    )(mine, theirs)


def second_kernel(*refs):
    for i, ref in enumerate(refs[:-1]):
        refs[-1][i] = ref[1]


def second_blocks(*pieces):
    shape = jax.ShapeDtypeStruct((len(pieces),) + pieces[0].shape[1:], pieces[0].dtype)
    return pl.pallas_call(
        second_kernel,
        in_specs=[VMEM] * len(pieces),
        out_specs=VMEM,
        out_shape=shape,
        compiler_params=pltpu.CompilerParams(vmem_limit_bytes=16 * 2**20),
    )(*pieces)


def transform_kernel(*refs, skip, far, steps, width, added):
    table_ref, tables_ref, *refs = refs[skip:]
    if far:
        blocks = [(r.at[0], r.at[1]) for r in refs[: 2 * len(steps)]]
        refs = refs[2 * len(steps) :]
    else:
        own, theirs, *came, changed = refs[:10]
        blocks = [(own, theirs.at[0])]
        for d, r in zip(NEAR[1:], came):
            blocks.append((r.at[0], changed.at[EARLY.index(d)] if d in EARLY else r.at[1]))
        refs = refs[10:]
    before = refs[0] if added else None
    out_ref, held = refs[-2:]
    me = here()
    core, z = (me >> 2) & 1, me & 3
    x = (me >> 3) & 1 ^ (1 if far else 0)
    sign = jnp.where(me < Y, 1.0, -1.0).astype(jnp.float32)
    levs, channels = held.shape[2], held.shape[3] // 8
    whole = 2 * (WIDE + REST)

    def put(e, lev, row, lane, value):
        for i in range(value.shape[1] // 128):
            held[e, lane // 128 + i, lev, pl.ds(row, 8), :] = value[:, i * 128 : (i + 1) * 128]

    def stage(flip):
        for j, step in enumerate(steps):
            lev = (z ^ step) & (levs - 1)

            def both(half, at, size):
                a = blocks[j][half ^ flip][:, at : at + size].astype(jnp.float32)
                b = blocks[len(steps) + j][half ^ flip][:, at : at + size].astype(jnp.float32)
                return a + b, (a - b) * sign

            for half in range(2):
                for c in range(channels):
                    for e, value in enumerate(both(half, c * WIDE, WIDE)):
                        put(e, lev, c * 8, half * (WIDE + 2 * REST), value)
            for c in range(0, channels, 2):
                zero, one = [both(half, channels * WIDE + c * REST, 2 * REST) for half in range(2)]
                for e in range(2):
                    even = jnp.concatenate([zero[e][:, :REST], one[e][:, :REST]], 1)
                    odd = jnp.concatenate([zero[e][:, REST:], one[e][:, REST:]], 1)
                    put(e, lev, c * 8, WIDE, even)
                    put(e, lev, c * 8 + 8, WIDE, odd)

    for flip in range(2):
        pl.when(core == flip)(functools.partial(stage, flip))

    rows = levs * channels
    low = (z ^ steps[0]) < levs
    lanes = pl.ds(pl.multiple_of(x * whole, 128), whole)
    slot = lax.broadcasted_iota(jnp.int32, table_ref.shape, 1) - me * 4
    for s in range(4):
        pair = jnp.sum(jnp.where(slot == s, table_ref[...], 0), axis=1, keepdims=True)
        for e in range(2):
            tiles = [held.at[e, i].reshape(rows * 8, 128) for i in range(whole // 128)]
            picked = [
                jnp.concatenate([t[pl.ds(2 * s + w, rows, stride=8), :] for t in tiles], 1)
                for w in range(2)
            ]
            products = lax.dot_general(
                jnp.concatenate(picked, 0).astype(jnp.bfloat16),
                tables_ref[s, e, :, lanes],
                NT,
                preferred_element_type=jnp.float32,
            )
            count = (width - pair - e + 1) >> 1
            degree = lax.broadcasted_iota(jnp.int32, (rows, products.shape[1]), 1)
            chosen = jnp.where(degree < count, products[:rows], products[rows:])
            if levs < 4:
                parts = [jnp.where(low, chosen, 0.0), jnp.where(low, 0.0, chosen)]
                chosen = jnp.concatenate(parts, 0)
            if added:
                chosen = chosen + before[s, e]
            out_ref[s, e] = chosen.astype(out_ref.dtype)


def transform(table, tables, blocks, far, steps, width, before=None, last=False, rest=()):
    slots, _, degrees, lats = tables.shape
    channels = blocks[0].shape[-1] // (WIDE + REST)
    more = [] if before is None else [before]
    return pl.pallas_call(
        functools.partial(
            transform_kernel,
            skip=len(rest),
            far=far,
            steps=steps,
            width=width,
            added=before is not None,
        ),
        in_specs=[pl.BlockSpec(memory_space=pl.ANY)] * len(rest)
        + [VMEM] * (2 + len(blocks) + len(more)),
        out_specs=VMEM,
        out_shape=jax.ShapeDtypeStruct(
            (slots, 2, 4 * channels, degrees), jnp.bfloat16 if last else jnp.float32
        ),
        scratch_shapes=[
            pltpu.VMEM((2, 2 * (WIDE + REST) // 128, len(steps), channels * 8, 128), jnp.float32)
        ],
        compiler_params=pltpu.CompilerParams(vmem_limit_bytes=20 * 2**20),
    )(*rest, table, tables, *blocks, *more)


def send(piece, distance):
    count = lax.axis_size("lat") * lax.axis_size("lev")
    return lax.ppermute(piece, ("lat", "lev"), [(i, i ^ distance) for i in range(count)])


def on_block(fourier, table, legendre):
    width = fourier.shape[2]
    entries = table.reshape(1, -1)
    mine, theirs, own, *early = pick(entries, fourier.transpose(1, 0, 2))
    got = {d: send(piece, d) for d, piece in zip(EARLY, early)}
    theirs = send(theirs, CORE)
    ready = dict(zip(JOINED, join(mine, theirs)))
    got.update({d: send(ready[d], d) for d in ORDER})
    came = [got[d] for d in EARLY]
    *came, got[ORDER[0]] = lax.optimization_barrier((*came, got[ORDER[0]]))
    changed = send(second_blocks(*came), CORE)
    near = [own, theirs] + [got[d] for d in NEAR[1:]] + [changed]
    total = transform(entries, legendre, near, False, (0, 1, 2, 3), width)
    far = [got[d] for d in FAR]
    rest = list(got.values())
    rest.insert(len(rest) - LATE, changed)
    return transform(
        entries, legendre, far, True, (0, 1, 2, 3), width, total, True, rest
    )


def row_counts(table, slot_count, wavenumbers):
    position = lax.axis_index(("lat", "lev")) * slot_count
    owned = lax.dynamic_slice_in_dim(table, position, slot_count)
    parity = jnp.arange(2, dtype=jnp.int32)
    return (wavenumbers - owned[:, None] - parity[None, :] + 1) // 2


def on_any(fourier, table, legendre):
    lat_count, lev_count = lax.axis_size("lat"), lax.axis_size("lev")
    devices, half_lat = lat_count * lev_count, lat_count // 2
    lat_rows, channels, wavenumbers = fourier.shape
    slot_count, _, degree_rows, _ = legendre.shape
    columns = jnp.stack([table, wavenumbers - 1 - table], axis=1).reshape(-1)
    picked = jnp.take(fourier, columns, axis=2)
    shaped = picked.reshape((1, lat_rows, channels, devices, wavenumbers // devices))
    arrived = lax.all_to_all(shaped, ("lat", "lev"), split_axis=3, concat_axis=0, tiled=True)
    halves = arrived.reshape(2, half_lat, lev_count, lat_rows, channels, slot_count, 2)
    north, south = halves[0].astype(jnp.float32), halves[1].astype(jnp.float32)
    merged = jnp.stack([north + south, north - south]).astype(jnp.bfloat16)
    tables = legendre.reshape(slot_count, 2, degree_rows, half_lat, lat_rows)
    products = jnp.einsum(
        "ealbcsw,serab->selcwr", merged, tables, preferred_element_type=jnp.float32
    )
    products = products.reshape(slot_count, 2, lev_count * channels, 2, degree_rows)
    first = row_counts(table, slot_count, wavenumbers)
    in_first = jnp.arange(degree_rows, dtype=jnp.int32)[None, None, :] < first[:, :, None]
    spectral = jnp.where(in_first[:, :, None, :], products[:, :, :, 0], products[:, :, :, 1])
    return spectral.astype(jnp.bfloat16)


def solution(mesh):
    in_specs = (P("lat", "lev", None), P(), P(("lat", "lev"), None, None, None))
    out_specs = P(("lat", "lev"), None, None, None)
    on_device = on_block if dict(mesh.shape) == {"lat": 8, "lev": 4} else on_any
    return jax.shard_map(
        on_device, mesh=mesh, in_specs=in_specs, out_specs=out_specs, check_vma=False
    )
```
